32 devices in a mesh: section: 2 (over core), dp: 4 (over y, x), tensor: 4 (over z).
Axes of the slice: x: 2, y: 2, z: 4, core: 2. Of those that a mesh axis runs over, the one named last changes fastest.
Arguments:
- tokens_in: bfloat16 [2, 1536, 2048], P(None, ('dp', 'tensor')), may hold values from -6 to 6
- cotangent: bfloat16 [2, 1536, 2048], P(None, ('dp', 'tensor')), may hold values from -6 to 6
- lengths: int32 [2, 4, 2], P(None, 'dp'), may hold values from 1 to 288, 384 in all within a row
- attn_gain: bfloat16 [2, 2048], P('section', 'dp'), may hold values from 0.5 to 1.5
- w_query: bfloat16 [2, 2048, 2048], P('section', 'dp', 'tensor'), may hold values from -0.125 to 0.125
- w_key: bfloat16 [2, 2048, 256], P('section', 'dp', 'tensor'), may hold values from -0.125 to 0.125
- w_value: bfloat16 [2, 2048, 256], P('section', 'dp', 'tensor'), may hold values from -0.125 to 0.125
- w_out: bfloat16 [2, 2048, 2048], P('section', 'tensor', 'dp'), may hold values from -1 to 1
- ffn_gain: bfloat16 [2, 2048], P('section', 'dp'), may hold values from 0.5 to 1.5
- w_gate: bfloat16 [2, 2048, 5632], P('section', 'dp', 'tensor'), may hold values from -0.125 to 0.125
- w_up: bfloat16 [2, 2048, 5632], P('section', 'dp', 'tensor'), may hold values from -0.125 to 0.125
- w_down: bfloat16 [2, 5632, 2048], P('section', 'tensor', 'dp'), may hold values from -0.078125 to 0.078125
Outputs:
- section_out: bfloat16 [2, 2, 1536, 2048], P('section', None, ('dp', 'tensor'))
- input_grad: bfloat16 [2, 2, 1536, 2048], P('section', None, ('dp', 'tensor'))
- grad_attn_gain: float32 [2, 2048], P('section', ('dp', 'tensor'))
- grad_query: float32 [2, 2048, 2048], P('section', 'dp', 'tensor')
- grad_key: float32 [2, 2048, 256], P('section', 'dp', 'tensor')
- grad_value: float32 [2, 2048, 256], P('section', 'dp', 'tensor')
- grad_out: float32 [2, 2048, 2048], P('section', 'tensor', 'dp')
- grad_ffn_gain: float32 [2, 2048], P('section', ('dp', 'tensor'))
- grad_gate: float32 [2, 2048, 5632], P('section', 'dp', 'tensor')
- grad_up: float32 [2, 2048, 5632], P('section', 'dp', 'tensor')
- grad_down: float32 [2, 5632, 2048], P('section', 'tensor', 'dp')
The draws below stay inside these ranges and needn't reach their ends.
Inputs may be any that keep to these rules, and one draw needn't show every extreme that they name: lengths[m, g, :] are the lengths of the sequences that fill the 384 rows of group g in micro-batch m, in order, summing to 384; each such row of lengths holds two sequences of 96 to 288 rows each.
All inputs are finite; a program needn't handle non-finite values.
Results may differ from the reference program's by a relative error of at most 0.03.
Values may be sent and summed in bfloat16 or wider, within the bound.
No kernel may reach another device: no remote copies, remote signals or barrier semaphores. Data moves between devices by JAX's collectives and lax.ppermute only.
A program may use at most 192 MiB of HBM per device.

```python
import math
import jax
import jax.numpy as jnp
import numpy as np
from jax import lax

D = 2048
HEAD = 64
FF = 5632
MICRO = 2
SEQS = 2
GROUP = 384
MOST = 288
TOKENS = 1536
HQ = 2048
KVD = 256
N_SECTION = 2
N_DP = 4


def level_of(own_key, extent, cuts, low, largest):
    def one(axis_at, parts):
        steps = jax.random.uniform(jax.random.fold_in(jax.random.fold_in(own_key, 6), axis_at), (parts,), jnp.float32, low / len(cuts), largest / len(cuts))
        return jnp.repeat(jnp.exp(steps), extent[axis_at] // parts).reshape((-1,) + (1,) * (len(extent) - axis_at - 1))

    factor_of = one(*cuts[0])
    for cut in cuts[1:]:
        factor_of = factor_of * one(*cut)
    return factor_of


def split_up(count, total, most, lean):
    portions = [(1 << 20) // math.isqrt(grade ** lean) + 1 for grade in range(2, count + 1)]
    surplus, holding = total - most - (count - 1), [1] * (count - 1)
    while surplus > 0:
        candidates = [i for i in range(count - 1) if holding[i] < most]
        pool, left = sum([portions[i] for i in candidates]), surplus
        for i in candidates:
            more = min(most - holding[i], max(1, left * portions[i] // pool), surplus)
            holding[i] = holding[i] + more
            surplus = surplus - more
    return np.array([most] + holding)


def ragged_sizes(stream_key, number_of, total, reach, slope):
    if number_of == 2:
        one = jax.random.randint(stream_key, (), max(1, total - reach), min(reach, total - 1) + 1)
        return jnp.stack([one, total - one])
    sizes = jnp.asarray(split_up(number_of, total, reach, slope), jnp.int32)
    twos = (number_of - 1) // 2
    source_of, taker = sizes[1:1 + 2 * twos:2], sizes[2:2 + 2 * twos:2]
    margin = jnp.minimum(source_of - 1, reach - taker)
    shifted = jax.random.randint(jax.random.fold_in(stream_key, 1), (twos,), 0, 1 << 20) % (margin + 1)
    sizes = sizes.at[1:1 + 2 * twos:2].set(source_of - shifted).at[2:2 + 2 * twos:2].set(taker + shifted)
    return sizes[jax.random.permutation(jax.random.fold_in(stream_key, 2), number_of)]


def bell_draw(own_key, shape, deviation, most, cuts=(), kind=jnp.bfloat16):
    values = jax.random.normal(own_key, shape, jnp.float32) * deviation
    if len(cuts) > 0:
        values = level_of(own_key, shape, cuts, -0.22, 0.18) * values
    return jnp.clip(values, min=-most, max=most).astype(kind)


def setup_inputs(seed: int = 0) -> dict:
    key_list = jax.random.split(jax.random.key(seed), 13)
    tokens_in = bell_draw(key_list[0], (MICRO, TOKENS, D), 1.0, 6.0, ((1, 16),))
    cotangent = bell_draw(key_list[1], (MICRO, TOKENS, D), 1.0, 6.0, ((1, 16),))
    lengths = jax.vmap(lambda own: ragged_sizes(own, SEQS, GROUP, MOST, 2))(jax.random.split(key_list[2], MICRO * N_DP)).reshape((MICRO, N_DP, SEQS)).astype(jnp.int32)
    attn_gain = jnp.clip(1.0 + 0.1 * jax.random.normal(key_list[3], (N_SECTION, D), jnp.float32), 0.5, 1.5).astype(jnp.bfloat16)
    w_query = bell_draw(key_list[4], (N_SECTION, D, HQ), D ** -0.5, 0.125, ((0, 2), (1, 4), (2, 4)))
    w_key = bell_draw(key_list[5], (N_SECTION, D, KVD), D ** -0.5, 0.125, ((0, 2), (1, 4), (2, 4)))
    w_value = bell_draw(key_list[6], (N_SECTION, D, KVD), D ** -0.5, 0.125, ((0, 2), (1, 4), (2, 4)))
    w_out = bell_draw(key_list[7], (N_SECTION, HQ, D), (D // 64) ** -0.5, 1.0, ((0, 2), (1, 4), (2, 4)))
    ffn_gain = jnp.clip(1.0 + 0.1 * jax.random.normal(key_list[8], (N_SECTION, D), jnp.float32), 0.5, 1.5).astype(jnp.bfloat16)
    w_gate = bell_draw(key_list[9], (N_SECTION, D, FF), D ** -0.5, 0.125, ((0, 2), (1, 4), (2, 4)))
    w_up = bell_draw(key_list[10], (N_SECTION, D, FF), D ** -0.5, 0.125, ((0, 2), (1, 4), (2, 4)))
    w_down = bell_draw(key_list[11], (N_SECTION, FF, D), FF ** -0.5, 0.078125, ((0, 2), (1, 4), (2, 4)))
    return dict(tokens_in=tokens_in, cotangent=cotangent, lengths=lengths, attn_gain=attn_gain, w_query=w_query, w_key=w_key, w_value=w_value, w_out=w_out, ffn_gain=ffn_gain, w_gate=w_gate, w_up=w_up, w_down=w_down)


@jax.custom_vjp
def low(v):
    return lax.optimization_barrier(v.astype(jnp.bfloat16)).astype(jnp.float32)

@jax.custom_vjp
def low_back(v):
    return v

def low_keep(v):
    return (low(v), None)

def low_pass(kept, grad):
    return (grad,)

def back_keep(v):
    return (v, None)

def back_low(kept, grad):
    return (low(grad),)
low.defvjp(low_keep, low_pass)
low_back.defvjp(back_keep, back_low)
EPSILON = 1e-05
MASK_FILL = -1e+30
HIGHEST = lax.Precision.HIGHEST

def matmul_high(left, right):
    return jnp.dot(left, right, precision=HIGHEST)

def sequence_layout(seq_lens, group):
    row_ids = jnp.arange(group, dtype=jnp.int32)
    ends = jnp.cumsum(seq_lens).astype(jnp.int32)
    starts = ends - seq_lens
    member = lax.optimization_barrier(jnp.sum((row_ids[:, None] >= ends[None, :]).astype(jnp.int32), axis=1))
    slots = jnp.arange(seq_lens.shape[0], dtype=jnp.int32)
    begins = lax.optimization_barrier(jnp.sum(jnp.where(member[:, None] == slots[None, :], starts[None, :], 0), axis=1))
    return (member, row_ids - begins)

def rotary_tables(position, head_size):
    half_dim = head_size // 2
    frequency = 10000.0 ** (-jnp.arange(half_dim, dtype=jnp.float32) / half_dim)
    angle_table = position.astype(jnp.float32)[:, None] * frequency[None, :]
    return (jnp.cos(angle_table), jnp.sin(angle_table))

def rotate(tensor, cosine, sine_part):
    half_dim = tensor.shape[-1] // 2
    front = tensor[..., :half_dim]
    back_half = tensor[..., half_dim:]
    return jnp.concatenate([front * cosine - back_half * sine_part, back_half * cosine + front * sine_part], axis=-1)

def normalize(tensor, gain_vec):
    return tensor * lax.rsqrt(lax.optimization_barrier(jnp.mean(tensor * tensor, axis=-1, keepdims=True)) + EPSILON) * gain_vec

def attend(block):
    queries, key_heads, value_heads, seq_lens = block
    group = queries.shape[0]
    member, position = sequence_layout(seq_lens, group)
    cosine, sine_part = rotary_tables(position, HEAD)
    queries = low(rotate(low_back(queries), cosine[:, None, :], sine_part[:, None, :]))
    key_heads = low(rotate(low_back(key_heads), cosine[:, None, :], sine_part[:, None, :]))
    value_heads = low(low_back(value_heads))
    kv_count = key_heads.shape[1]
    repeats = queries.shape[1] // kv_count
    queries = queries.reshape(group, kv_count, repeats, HEAD)
    scores = low_back(jnp.einsum('qgrd,kgd->grqk', queries, key_heads, precision=HIGHEST) * HEAD ** (-0.5))
    row_ids = jnp.arange(group, dtype=jnp.int32)
    allowed = (member[:, None] == member[None, :]) & (row_ids[:, None] >= row_ids[None, :])
    scores = jnp.where(allowed, scores, MASK_FILL)
    row_max = lax.optimization_barrier(jnp.max(scores, axis=-1, keepdims=True))
    exponent = jnp.exp(scores - row_max)
    softmax_probs = low(exponent / lax.optimization_barrier(jnp.sum(exponent, axis=-1, keepdims=True)))
    mixed = jnp.einsum('grqk,kgd->qgrd', softmax_probs, value_heads, precision=HIGHEST)
    return mixed.reshape(group, kv_count * repeats * HEAD)

def layer(layer_in, lengths, norm_gain, w_query, w_key, w_value, w_out, ffn_gain, w_gate, w_up, w_down):
    shape_in = layer_in.shape
    row_block = low_back(layer_in.reshape(-1, shape_in[-1]))
    normed_one = low(normalize(row_block, norm_gain))
    queries = matmul_high(normed_one, w_query)
    key_heads = matmul_high(normed_one, w_key)
    value_heads = matmul_high(normed_one, w_value)
    blocks = shape_in[0] * (shape_in[1] // GROUP)
    mixed = lax.map(jax.checkpoint(attend), (queries.reshape(blocks, GROUP, -1, HEAD), key_heads.reshape(blocks, GROUP, -1, HEAD), value_heads.reshape(blocks, GROUP, -1, HEAD), lengths.reshape(blocks, -1)))
    mixed = low(low_back(mixed.reshape(row_block.shape[0], -1)))
    middle = row_block + low_back(matmul_high(mixed, w_out))
    normed_two = low(normalize(middle, ffn_gain))
    gate_proj = low_back(matmul_high(normed_two, w_gate))
    up_proj = low_back(matmul_high(normed_two, w_up))
    hidden = low(jax.nn.silu(gate_proj) * up_proj)
    result = middle + low_back(matmul_high(hidden, w_down))
    return low(result).reshape(shape_in)

def reference(tokens_in, cotangent, lengths, attn_gain, w_query, w_key, w_value, w_out, ffn_gain, w_gate, w_up, w_down):
    stacks = (attn_gain, w_query, w_key, w_value, w_out, ffn_gain, w_gate, w_up, w_down)

    def run_layer(layer_in, *params):
        return layer(layer_in, lengths, *params)
    first_params = [param_stack[0].astype(jnp.float32) for param_stack in stacks]
    second_params = [param_stack[1].astype(jnp.float32) for param_stack in stacks]
    first_out, first_back = jax.vjp(run_layer, tokens_in.astype(jnp.float32), *first_params)
    second_out, second_back = jax.vjp(run_layer, first_out, *second_params)
    second_grads = second_back(cotangent.astype(jnp.float32))
    first_grads = first_back(second_grads[0])
    paired = [jnp.stack([first_grads[which], second_grads[which]]) for which in range(1, 10)]
    section_out = jnp.stack([first_out, second_out]).astype(jnp.bfloat16)
    input_grad = jnp.stack([first_grads[0], second_grads[0]]).astype(jnp.bfloat16)
    return (section_out, input_grad, paired[0], paired[1], paired[2], paired[3], paired[4], paired[5], paired[6], paired[7], paired[8])
```

```python
import jax
import jax.numpy as jnp
from jax import lax
from jax.experimental import pallas as pl
from jax.experimental.pallas import tpu as pltpu
from jax.sharding import PartitionSpec as P

HEAD = 64


EPSILON = 1e-05
MASK_FILL = -1e30
BF16 = jnp.bfloat16
F32 = jnp.float32
LANES = 128
SCALE = HEAD ** (-0.5)
VMEM_BYTES = 24 * 2**20


def turn(value, axis, steps):
    count = lax.axis_size(axis)
    return lax.ppermute(value, axis, [(i, (i + steps) % count) for i in range(count)])


def swap(value):
    return lax.ppermute(value, "section", [(0, 1), (1, 0)])


def contract(left, right, left_dim, right_dim):
    return lax.dot_general(
        left, right, (((left_dim,), (right_dim,)), ((), ())), preferred_element_type=F32
    )


def geometry(seq_lens, rows):
    count = lax.axis_size("tensor")
    place = (lax.axis_index("tensor") - jnp.arange(count, dtype=jnp.int32)) % count
    row_ids = (place[:, None] * rows + jnp.arange(rows, dtype=jnp.int32)[None, :]).reshape(-1)
    ends = jnp.cumsum(seq_lens)
    starts = ends - seq_lens
    member = jnp.sum((row_ids[:, None] >= ends[None, :]).astype(jnp.int32), axis=1)
    slots = jnp.arange(seq_lens.shape[0], dtype=jnp.int32)
    begins = jnp.sum(jnp.where(member[:, None] == slots[None, :], starts[None, :], 0), axis=1)
    position = row_ids - begins
    half_dim = HEAD // 2
    frequency = 10000.0 ** (-jnp.arange(half_dim, dtype=F32) / half_dim)
    angle = position.astype(F32)[:, None] * frequency[None, :]
    allowed = (member[:, None] == member[None, :]) & (row_ids[:, None] >= row_ids[None, :])
    cosine, sine_part = (jnp.cos(angle), jnp.sin(angle))
    cosine = jnp.concatenate([cosine] * (LANES // half_dim), axis=1)
    sine_part = jnp.concatenate([-sine_part, sine_part] * (LANES // HEAD), axis=1)
    turned = jnp.arange(LANES) < HEAD
    tables = jnp.stack(
        [cosine, sine_part, jnp.where(turned, cosine, 1.0), jnp.where(turned, sine_part, 0.0)]
    )
    return (tables, jnp.where(allowed, 0.0, MASK_FILL))


def barrier(*values):
    return lax.optimization_barrier(values)


class Job:
    def __init__(self, fn, *inputs):
        self.fn, self.inputs, self.results = (fn, inputs, None)

    def __getitem__(self, which):
        return self.results[which]


def step(value, job):
    if job is None:
        return turn(value, "tensor", 1)
    inputs = job.inputs() if callable(job.inputs) else job.inputs
    value, *inputs = barrier(value, *inputs)
    recv = turn(value, "tensor", 1)
    recv, *results = barrier(recv, *job.fn(*inputs))
    job.results = results
    return recv


def spread(block, jobs=()):
    pieces = [block]
    for k in range(lax.axis_size("tensor") - 1):
        pieces.append(step(pieces[-1], jobs[k] if k < len(jobs) else None))
    return jnp.concatenate(pieces, axis=0)


def collect(partial, jobs=()):
    count = lax.axis_size("tensor")
    rows = partial.shape[0] // count
    blocks = partial.reshape(count, rows, partial.shape[1])
    total = blocks[1 % count]
    for k in range(count - 1):
        recv = step(total.astype(BF16), jobs[k] if k < len(jobs) else None)
        total = recv.astype(F32) + blocks[(k + 2) % count]
    return total


class Ring:
    def __init__(self, first):
        self.count, self.taken, self.value = (lax.axis_size("tensor"), 0, first)

    def run(self, fn, *inputs):
        if self.taken == self.count - 1:
            return fn(*inputs)
        job = Job(fn, *inputs)
        self.accept(step(self.value, job))
        self.taken += 1
        return tuple(job.results)

    def finish(self):
        while self.taken < self.count - 1:
            self.run(lambda: ())
        return self.result()


class SpreadRing(Ring):
    def __init__(self, block):
        super().__init__(block)
        self.pieces = [block]

    def accept(self, recv):
        self.pieces.append(recv)
        self.value = recv

    def result(self):
        return jnp.concatenate(self.pieces, axis=0)


class CollectRing(Ring):
    def __init__(self, partial):
        count = lax.axis_size("tensor")
        self.blocks = partial.reshape(count, partial.shape[0] // count, partial.shape[1])
        self.total = self.blocks[1 % count].astype(F32)
        super().__init__(self.total.astype(BF16))

    def accept(self, recv):
        self.total = recv.astype(F32) + self.blocks[(self.taken + 2) % self.count]
        self.value = self.total.astype(BF16)

    def result(self):
        return self.total


def gather_direct(piece):
    count, me = (lax.axis_size("dp"), lax.axis_index("dp"))
    whole = jnp.zeros((count,) + piece.shape, piece.dtype)
    for k in range(count):
        part = turn(piece, "dp", k) if k else piece
        whole = lax.dynamic_update_index_in_dim(whole, part, (me - k) % count, 0)
    return whole


def normalizer(rows):
    return lax.rsqrt(jnp.mean(rows * rows, axis=1, keepdims=True) + EPSILON)


def half_swap(x):
    lane = lax.broadcasted_iota(jnp.int32, x.shape, 1)
    first = (lane % HEAD) < HEAD // 2
    return jnp.where(
        first, pltpu.roll(x, LANES - HEAD // 2, 1), pltpu.roll(x, HEAD // 2, 1)
    )


def heads_of(kv):
    low = lax.broadcasted_iota(jnp.int32, kv.shape, 1) < HEAD
    kv = kv.astype(F32)
    turned = pltpu.roll(kv, HEAD, 1)
    keys = (jnp.where(low, kv, 0.0).astype(BF16), jnp.where(low, 0.0, turned).astype(BF16))
    values = (jnp.where(low, turned, 0.0).astype(BF16), jnp.where(low, 0.0, kv).astype(BF16))
    return (keys, values)


def attend_kernel(qkv_ref, table_ref, bias_ref, rot_ref, mixed_ref, lse_ref):
    q_cols = mixed_ref.shape[1]
    cosine, sine_part = (table_ref[0], table_ref[1])
    kv = qkv_ref[:, q_cols:]
    kv = (kv * table_ref[2] + half_swap(kv) * table_ref[3]).astype(BF16)
    rot_ref[:, q_cols:] = kv
    keys, values = heads_of(kv)
    bias = bias_ref[...]
    log_totals = []
    for slab in range(q_cols // LANES):
        cols = slice(slab * LANES, (slab + 1) * LANES)
        query = qkv_ref[:, cols]
        query = (query * cosine + half_swap(query) * sine_part).astype(BF16)
        rot_ref[:, cols] = query
        mixed = 0.0
        for odd in range(2):
            scores = contract(query, keys[odd], 1, 1) * SCALE + bias
            row_max = jnp.max(scores, axis=1, keepdims=True)
            exponent = jnp.exp(scores - row_max)
            totals = jnp.sum(exponent, axis=1, keepdims=True)
            log_totals.append(row_max + jnp.log(totals))
            mixed = mixed + contract((exponent / totals).astype(BF16), values[odd], 1, 0)
        mixed_ref[:, cols] = mixed.astype(BF16)
    lse_ref[...] = jnp.concatenate(log_totals, axis=1)


def attend(normed_one, geo, w_attn, kv_cols):
    group = normed_one.shape[0]
    q_cols = w_attn.shape[1] // 2 - kv_cols
    both = q_cols + 2 * kv_cols
    qkv = jnp.dot(normed_one, w_attn[:, :both], preferred_element_type=F32)
    rotated, mixed, log_total = pl.pallas_call(
        attend_kernel,
        out_shape=(
            jax.ShapeDtypeStruct((group, both), BF16),
            jax.ShapeDtypeStruct((group, q_cols), BF16),
            jax.ShapeDtypeStruct((group, q_cols // HEAD), F32),
        ),
        compiler_params=pltpu.CompilerParams(vmem_limit_bytes=VMEM_BYTES),
    )(qkv, *geo)
    return (contract(mixed, w_attn[:, both:], 1, 1), rotated, log_total, mixed)


def attend_back_kernel(d_mixed_ref, rot_ref, lse_ref, table_ref, bias_ref, out_ref):
    q_cols = d_mixed_ref.shape[1]
    cosine, sine_part = (table_ref[0], table_ref[1])
    keys, values = heads_of(rot_ref[:, q_cols:])
    bias = bias_ref[...]
    d_keys = [0.0, 0.0]
    d_values = [0.0, 0.0]
    for slab in range(q_cols // LANES):
        cols = slice(slab * LANES, (slab + 1) * LANES)
        query = rot_ref[:, cols]
        d_mixed = d_mixed_ref[:, cols]
        d_query = 0.0
        for odd in range(2):
            head = 2 * slab + odd
            scores = contract(query, keys[odd], 1, 1) * SCALE + bias
            probs = jnp.exp(scores - lse_ref[:, head : head + 1])
            d_probs = contract(d_mixed, values[odd], 1, 1)
            total = jnp.sum(d_probs * probs, axis=1, keepdims=True)
            d_scores = (probs * (d_probs - total)).astype(BF16)
            d_query = d_query + contract(d_scores, keys[odd], 1, 0)
            d_values[odd] = d_values[odd] + contract(probs.astype(BF16), d_mixed, 0, 0)
            d_keys[odd] = d_keys[odd] + contract(d_scores, query, 0, 0)
        d_query = d_query * SCALE
        out_ref[:, cols] = (d_query * cosine - half_swap(d_query) * sine_part).astype(BF16)
    low = lax.broadcasted_iota(jnp.int32, d_keys[0].shape, 1) < HEAD
    d_kv = jnp.where(
        low,
        (d_keys[0] + pltpu.roll(d_keys[1], HEAD, 1)) * SCALE,
        d_values[1] + pltpu.roll(d_values[0], HEAD, 1),
    )
    d_kv = d_kv * table_ref[2] - half_swap(d_kv) * table_ref[3]
    out_ref[:, q_cols:] = d_kv.astype(BF16)


def attend_back(grad_attn, geo, w_attn, rotated, log_total):
    both = rotated.shape[1]
    d_mixed = jnp.dot(grad_attn, w_attn[:, both:], preferred_element_type=F32).astype(BF16)
    d_qkv = pl.pallas_call(
        attend_back_kernel,
        out_shape=jax.ShapeDtypeStruct(rotated.shape, BF16),
        compiler_params=pltpu.CompilerParams(vmem_limit_bytes=VMEM_BYTES),
    )(d_mixed, rotated, log_total, *geo)
    return (d_qkv, contract(d_qkv, w_attn[:, :both], 1, 1))


def feed(normed_two, w_ffn, units):
    gate_up = jnp.dot(normed_two, w_ffn[:, : 2 * units], preferred_element_type=F32)
    hidden = (jax.nn.silu(gate_up[:, :units]) * gate_up[:, units:]).astype(BF16)
    return (gate_up, hidden)


def feed_back(grad_feed, gate_up, w_ffn, w_down):
    units = gate_up.shape[1] // 2
    d_hidden = jnp.dot(grad_feed, w_down[:, -units:], preferred_element_type=F32)
    gate, up = (gate_up[:, :units], gate_up[:, units:])
    sigmoid_gate = jax.nn.sigmoid(gate)
    d_up = (d_hidden * gate * sigmoid_gate).astype(BF16)
    d_gate = (d_hidden * up * sigmoid_gate * (1.0 + gate * (1.0 - sigmoid_gate))).astype(BF16)
    d_gate_up = jnp.concatenate([d_gate, d_up], axis=1)
    return (d_gate_up, contract(d_gate_up, w_ffn[:, : 2 * units], 1, 1))


def core_half(rows, at_first, own):
    width = rows.shape[1] // (2 * lax.axis_size("dp"))
    low, high = (
        jnp.concatenate(
            [rows[:, start : start + width] for start in range(first, rows.shape[1], 2 * width)],
            axis=1,
        )
        for first in (0, width)
    )
    return jnp.where(at_first, low, high) if own else jnp.where(at_first, high, low)


def sent_grad(rows, grads, at_first):
    return swap(contract(core_half(rows, at_first, False), grads, 0, 0).astype(BF16))


def kept_grad(rows, grads, got, at_first):
    kept = contract(core_half(rows, at_first, True), grads, 0, 0)
    return (kept + got.astype(F32)).astype(BF16)


def scatter(half):
    return lax.psum_scatter(half, "dp", scatter_dimension=0, tiled=True)


def norm_back(rows, inverse, gain, d_normed):
    unit = rows * inverse
    scaled = d_normed * gain
    return inverse * (scaled - unit * jnp.mean(scaled * unit, axis=1, keepdims=True))


def backward(
    kept, grad_feed, grad_result, geo, weights, at_first, layer_in, normed_one, aside, arriving
):
    (rotated, log_total, mixed, middle, normed_two, gate_up, hidden) = kept
    norm_gain, ffn_gain, w_attn, w_ffn, w_down = weights
    d_gate_up, d_norm_two_all = aside.run(feed_back, grad_feed, gate_up, w_ffn, w_down)
    ffn_sent = Job(
        lambda rows, grads, *rest: (sent_grad(rows, grads, at_first), *rest),
        normed_two,
        d_gate_up,
        *arriving,
    )
    ffn_kept = Job(lambda *given: (kept_grad(*given, at_first),))
    ffn_kept.inputs = lambda: (normed_two, d_gate_up, ffn_sent[0])
    down_sent = Job(lambda *given: (sent_grad(*given, at_first),), grad_feed, hidden)
    d_norm_two = collect(d_norm_two_all, (ffn_sent, ffn_kept, down_sent))
    r_ffn = scatter(ffn_kept[0])
    d_middle = grad_result + norm_back(middle, normalizer(middle), ffn_gain, d_norm_two)
    down_kept = Job(lambda *given: (kept_grad(*given, at_first),))
    down_kept.inputs = lambda: (grad_feed, hidden, down_sent[0])
    ffn_gain_job = Job(
        lambda d_all, normed: (jnp.sum(d_all * (normed.astype(F32) / ffn_gain), axis=0),),
        d_norm_two_all,
        normed_two,
    )
    ffn_done = Job(lambda *given: given, r_ffn)
    grad_attn = spread(d_middle.astype(BF16), (down_kept, ffn_gain_job, ffn_done))
    r_down = scatter(down_kept[0])
    d_qkv, d_norm_one_all = aside.run(
        lambda grad_attn, w_attn, *rest: attend_back(grad_attn, geo, w_attn, *rest),
        grad_attn,
        w_attn,
        rotated,
        log_total,
    )
    attn_sent = Job(
        lambda rows, grads, above, heads: (
            sent_grad(rows, grads, at_first),
            sent_grad(above, heads, at_first),
        ),
        normed_one,
        d_qkv,
        grad_attn,
        mixed,
    )
    attn_kept = Job(
        lambda rows, grads, got, above, heads, got_out: (
            jnp.concatenate(
                [
                    kept_grad(rows, grads, got, at_first),
                    kept_grad(above, heads, got_out, at_first),
                ],
                axis=1,
            ),
        )
    )
    attn_kept.inputs = lambda: (normed_one, d_qkv, attn_sent[0], grad_attn, mixed, attn_sent[1])
    attn_gain_job = Job(
        lambda d_all, normed, done: (
            jnp.sum(d_all * (normed.astype(F32) / norm_gain), axis=0),
            done,
        ),
        d_norm_one_all,
        normed_one,
        r_down,
    )
    d_norm_one = collect(d_norm_one_all, (attn_sent, attn_kept, attn_gain_job))
    r_attn = scatter(attn_kept[0])
    d_input = d_middle + norm_back(layer_in, normalizer(layer_in), norm_gain, d_norm_one)
    return (
        d_input.astype(BF16),
        (r_attn, ffn_done[0], attn_gain_job[1]),
        jnp.stack([attn_gain_job[0], ffn_gain_job[0]]),
        ffn_sent.results[1:],
    )


def both_layers(own, at_first):
    rows = own.shape[0] // 2
    low, high = (own[:rows], own[rows:])
    mine = jnp.where(at_first, low, high)
    got = swap(jnp.where(at_first, high, low))
    return (jnp.where(at_first, mine, got), jnp.where(at_first, got, mine))


def own_layer(first, second, at_first):
    mine = jnp.where(at_first, first, second)
    got = swap(jnp.where(at_first, second, first))
    return jnp.concatenate([jnp.where(at_first, mine, got), jnp.where(at_first, got, mine)], axis=0)


def gather(shard):
    return lax.all_gather(shard, ("dp", "section"), axis=0, tiled=True)


def gather_small(piece):
    return gather_direct(piece).transpose(1, 0, 2).reshape(piece.shape[0], -1)


def reduce_small(rows):
    for axis in ("tensor", "dp"):
        count = lax.axis_size(axis)
        if axis == "tensor":
            parts = rows.reshape(rows.shape[0], lax.axis_size("dp"), count, -1).transpose(2, 0, 1, 3)
        else:
            parts = rows.transpose(1, 0, 2)
        me = lax.axis_index(axis)
        rows = lax.dynamic_index_in_dim(parts, me, 0, keepdims=False)
        for k in range(1, count):
            part = lax.dynamic_index_in_dim(parts, (me + k) % count, 0, keepdims=False)
            rows = rows + turn(part, axis, k)
    return rows + swap(rows)


def local(
    tokens_in,
    cotangent,
    lengths,
    attn_gain,
    w_query,
    w_key,
    w_value,
    w_out,
    ffn_gain,
    w_gate,
    w_up,
    w_down,
):
    at_first = lax.axis_index("section") == 0
    rows = tokens_in.shape[1]
    q_cols, kv_cols, units = (w_query.shape[2], w_key.shape[2], w_gate.shape[2])
    tokens = jnp.where(at_first, tokens_in[0], tokens_in[1])
    upstream = jnp.where(at_first, cotangent[0], cotangent[1])
    own_gains = jnp.concatenate([attn_gain, ffn_gain], axis=0)
    attn_rows = jnp.concatenate([w_query[0], w_key[0], w_value[0], w_out[0].T], axis=1)
    attn_rows, tokens = barrier(attn_rows, tokens)
    attn_parts = both_layers(attn_rows, at_first)

    def collect_gains(own):
        other = swap(own)
        own, other = (jnp.where(at_first, own, other), jnp.where(at_first, other, own))
        return (gather_small(jnp.concatenate([own, other])).astype(F32),)

    def prepare_ffn(gate, up, down):
        parts = both_layers(jnp.concatenate([gate, up, down.T], axis=1), at_first)
        return (parts[0][:, : 2 * units], parts[0][:, 2 * units :], parts[1])

    gains_job = Job(collect_gains, own_gains)
    prepare = Job(prepare_ffn, w_gate[0], w_up[0], w_down[0])
    tokens_all = spread(tokens, (prepare, gains_job))
    gains = gains_job[0]
    tokens_all, upstream = barrier(tokens_all, upstream)
    upstream_ring = SpreadRing(upstream)
    geo = geometry(jnp.where(at_first, lengths[0, 0], lengths[1, 0]), rows)
    tokens_all = tokens_all.astype(F32)
    layer_in = tokens.astype(F32)
    normed_one = (tokens_all * normalizer(tokens_all) * gains[0]).astype(BF16)

    def whole_down(half):
        got = swap(half)
        return (
            jnp.where(
                at_first, jnp.stack([half, got], axis=1), jnp.stack([got, half], axis=1)
            ).reshape(-1, half.shape[-1]),
        )

    w_attn, down_part, ffn_part = barrier(gather(attn_parts[0]), prepare[1], prepare[0])
    w_attns = [w_attn]
    w_ffns = [gather(ffn_part)]
    down_job = Job(whole_down, gather_direct(down_part))
    w_attns.append(gather(attn_parts[1]))
    w_ffns.append(gather(prepare[2]))
    layers = []
    for layer in range(2):
        norm_gain, ffn_gain = (gains[2 * layer], gains[2 * layer + 1])
        w_attn, w_ffn = (w_attns[layer], w_ffns[layer])
        if layer:
            normed_one = spread((layer_in * normalizer(layer_in) * norm_gain).astype(BF16))
        out_term, *attn_kept = upstream_ring.run(
            lambda normed, w: attend(normed, geo, w, kv_cols), normed_one, w_attn
        )
        middle = layer_in + collect(out_term)
        normed_two = spread(
            (middle * normalizer(middle) * ffn_gain).astype(BF16), () if layer else (None, down_job)
        )
        w_down_all = w_ffn if layer else down_job[0]
        gate_up, hidden = upstream_ring.run(
            lambda normed, w: feed(normed, w, units), normed_two, w_ffn
        )
        kept = (*attn_kept, middle, normed_two, gate_up, hidden)
        weights = (norm_gain, ffn_gain, w_attn, w_ffn, w_down_all)
        layers.append((kept, weights, layer_in, normed_one))
        if layer == 0:
            first_out = (middle + collect(contract(hidden, w_down_all[:, -units:], 1, 1))).astype(BF16)
            layer_in = first_out.astype(F32)
    upstream_all = upstream_ring.finish()
    out_ring = CollectRing(contract(hidden, w_down_all[:, -units:], 1, 1))

    def back(layer, grad_all, grad, arriving):
        kept, weights, layer_in, normed_one = layers[layer]
        return backward(
            kept,
            grad_all,
            grad.astype(F32),
            geo,
            weights,
            at_first,
            layer_in,
            normed_one,
            out_ring,
            arriving,
        )

    d_second, second_reduced, second_gains, _ = back(1, upstream_all, upstream, ())
    d_first, first_reduced, first_gains, second_attn = back(
        0, spread(d_second), d_second, second_reduced[:1]
    )
    second_out = (middle + out_ring.finish()).astype(BF16)
    second_reduced = (second_attn[0], *second_reduced[1:])
    g_attn, g_ffn, g_down = (
        own_layer(first, second, at_first).astype(F32)
        for first, second in zip(first_reduced, second_reduced)
    )
    g_gains = reduce_small(jnp.concatenate([first_gains, second_gains]))
    gain_own = jnp.where(at_first, g_gains[:2], g_gains[2:])
    results = (first_out, second_out)
    input_grads = (d_first, d_second)

    def by_layer(first, second):
        mine = jnp.where(at_first, first, second)
        got = swap(jnp.where(at_first, second, first))
        return jnp.stack([jnp.where(at_first, mine, got), jnp.where(at_first, got, mine)])

    section_out = by_layer(results[0], results[1])
    input_grad = by_layer(input_grads[0], input_grads[1])
    qkv = q_cols + 2 * kv_cols
    return (
        section_out[None],
        input_grad[None],
        gain_own[0][None],
        g_attn[:, :q_cols][None],
        g_attn[:, q_cols : q_cols + kv_cols][None],
        g_attn[:, q_cols + kv_cols : qkv][None],
        g_attn[:, qkv:].T[None],
        gain_own[1][None],
        g_ffn[:, :units][None],
        g_ffn[:, units:][None],
        g_down.T[None],
    )


def solution(mesh):
    return jax.shard_map(
        local,
        mesh=mesh,
        in_specs=(
            P(None, ("dp", "tensor"), None),
            P(None, ("dp", "tensor"), None),
            P(None, "dp", None),
            P("section", "dp"),
            P("section", "dp", "tensor"),
            P("section", "dp", "tensor"),
            P("section", "dp", "tensor"),
            P("section", "tensor", "dp"),
            P("section", "dp"),
            P("section", "dp", "tensor"),
            P("section", "dp", "tensor"),
            P("section", "tensor", "dp"),
        ),
        out_specs=(
            P("section", None, ("dp", "tensor"), None),
            P("section", None, ("dp", "tensor"), None),
            P("section", ("dp", "tensor")),
            P("section", "dp", "tensor"),
            P("section", "dp", "tensor"),
            P("section", "dp", "tensor"),
            P("section", "tensor", "dp"),
            P("section", ("dp", "tensor")),
            P("section", "dp", "tensor"),
            P("section", "dp", "tensor"),
            P("section", "tensor", "dp"),
        ),
        check_vma=False,
    )
```

```python
import jax
import jax.numpy as jnp
from jax import lax
from jax.experimental import pallas as pl
from jax.experimental.pallas import tpu as pltpu
from jax.sharding import PartitionSpec as P

HEAD = 64


EPSILON = 1e-05
MASK_FILL = -1e30
BF16 = jnp.bfloat16
F32 = jnp.float32
LANES = 128
SCALE = HEAD ** (-0.5)
VMEM_BYTES = 28 * 2**20


def turn(value, axis, steps):
    count = lax.axis_size(axis)
    return lax.ppermute(value, axis, [(i, (i + steps) % count) for i in range(count)])


def swap(value):
    return lax.ppermute(value, "section", [(0, 1), (1, 0)])


def contract(left, right, left_dim, right_dim):
    return lax.dot_general(
        left, right, (((left_dim,), (right_dim,)), ((), ())), preferred_element_type=F32
    )


def geometry(seq_lens, rows):
    count = lax.axis_size("tensor")
    place = (lax.axis_index("tensor") - jnp.arange(count, dtype=jnp.int32)) % count
    row_ids = (place[:, None] * rows + jnp.arange(rows, dtype=jnp.int32)[None, :]).reshape(-1)
    ends = jnp.cumsum(seq_lens)
    starts = ends - seq_lens
    member = jnp.sum((row_ids[:, None] >= ends[None, :]).astype(jnp.int32), axis=1)
    slots = jnp.arange(seq_lens.shape[0], dtype=jnp.int32)
    begins = jnp.sum(jnp.where(member[:, None] == slots[None, :], starts[None, :], 0), axis=1)
    position = row_ids - begins
    half_dim = HEAD // 2
    frequency = 10000.0 ** (-jnp.arange(half_dim, dtype=F32) / half_dim)
    angle = position.astype(F32)[:, None] * frequency[None, :]
    allowed = (member[:, None] == member[None, :]) & (row_ids[:, None] >= row_ids[None, :])
    cosine, sine_part = (jnp.cos(angle), jnp.sin(angle))
    cosine = jnp.concatenate([cosine] * (LANES // half_dim), axis=1)
    sine_part = jnp.concatenate([-sine_part, sine_part] * (LANES // HEAD), axis=1)
    turned = jnp.arange(LANES) < HEAD
    tables = jnp.stack(
        [cosine, sine_part, jnp.where(turned, cosine, 1.0), jnp.where(turned, sine_part, 0.0)]
    )
    return (tables, jnp.where(allowed, 0.0, MASK_FILL))


def barrier(*values):
    return lax.optimization_barrier(values)


class Job:
    def __init__(self, fn, *inputs, held=()):
        self.fn, self.inputs, self.held, self.results = (fn, inputs, held, None)

    def __getitem__(self, which):
        return self.results[which]


def step(value, job):
    if job is None:
        return turn(value, "tensor", 1)
    inputs = job.inputs() if callable(job.inputs) else job.inputs
    value, *inputs = barrier(value, *inputs)
    results = job.fn(*inputs)
    recv, *values = barrier(turn(value, "tensor", 1), *results, *job.held)
    job.results, job.held = (values[: len(results)], values[len(results) :])
    return recv


def spread(block, jobs=()):
    pieces = [block]
    for k in range(lax.axis_size("tensor") - 1):
        pieces.append(step(pieces[-1], jobs[k] if k < len(jobs) else None))
    return jnp.concatenate(pieces, axis=0)


def collect(partial, jobs=()):
    count = lax.axis_size("tensor")
    rows = partial.shape[0] // count
    blocks = partial.reshape(count, rows, partial.shape[1])
    total = blocks[1 % count]
    for k in range(count - 1):
        recv = step(total.astype(BF16), jobs[k] if k < len(jobs) else None)
        total = recv.astype(F32) + blocks[(k + 2) % count].astype(F32)
    return total


class Ring:
    def __init__(self, first):
        self.count, self.taken, self.value = (lax.axis_size("tensor"), 0, first)

    def run(self, fn, *inputs):
        if self.taken == self.count - 1:
            return fn(*inputs)
        job = Job(fn, *inputs)
        self.accept(step(self.value, job))
        self.taken += 1
        return tuple(job.results)

    def finish(self):
        while self.taken < self.count - 1:
            self.run(lambda: ())
        return self.result()


class SpreadRing(Ring):
    def __init__(self, block):
        super().__init__(block)
        self.pieces = [block]

    def accept(self, recv):
        self.pieces.append(recv)
        self.value = recv

    def result(self):
        return jnp.concatenate(self.pieces, axis=0)


class CollectRing(Ring):
    def __init__(self, partial):
        count = lax.axis_size("tensor")
        self.blocks = partial.reshape(count, partial.shape[0] // count, partial.shape[1])
        self.total = self.blocks[1 % count].astype(F32)
        super().__init__(self.total.astype(BF16))

    def accept(self, recv):
        block = self.blocks[(self.taken + 2) % self.count]
        self.total = recv.astype(F32) + block.astype(F32)
        self.value = self.total.astype(BF16)

    def result(self):
        return self.total


def normalizer(rows):
    return lax.rsqrt(jnp.mean(rows * rows, axis=1, keepdims=True) + EPSILON)


def half_swap(x):
    lane = lax.broadcasted_iota(jnp.int32, x.shape, 1)
    first = (lane % HEAD) < HEAD // 2
    return jnp.where(
        first, pltpu.roll(x, LANES - HEAD // 2, 1), pltpu.roll(x, HEAD // 2, 1)
    )


def heads_of(kv):
    low = lax.broadcasted_iota(jnp.int32, kv.shape, 1) < HEAD
    kv = kv.astype(F32)
    turned = pltpu.roll(kv, HEAD, 1)
    keys = (jnp.where(low, kv, 0.0).astype(BF16), jnp.where(low, 0.0, turned).astype(BF16))
    values = (jnp.where(low, turned, 0.0).astype(BF16), jnp.where(low, 0.0, kv).astype(BF16))
    return (keys, values)


def attend_kernel(qkv_ref, table_ref, bias_ref, rot_ref, mixed_ref, lse_ref):
    q_cols = mixed_ref.shape[1]
    cosine, sine_part = (table_ref[0], table_ref[1])
    kv = qkv_ref[:, q_cols:]
    kv = (kv * table_ref[2] + half_swap(kv) * table_ref[3]).astype(BF16)
    rot_ref[:, q_cols:] = kv
    keys, values = heads_of(kv)
    bias = bias_ref[...]
    log_totals = []
    for slab in range(q_cols // LANES):
        cols = slice(slab * LANES, (slab + 1) * LANES)
        query = qkv_ref[:, cols]
        query = (query * cosine + half_swap(query) * sine_part).astype(BF16)
        rot_ref[:, cols] = query
        mixed = 0.0
        for odd in range(2):
            scores = contract(query, keys[odd], 1, 1) * SCALE + bias
            row_max = jnp.max(scores, axis=1, keepdims=True)
            exponent = jnp.exp(scores - row_max)
            totals = jnp.sum(exponent, axis=1, keepdims=True)
            log_totals.append(row_max + jnp.log(totals))
            mixed = mixed + contract((exponent / totals).astype(BF16), values[odd], 1, 0)
        mixed_ref[:, cols] = mixed.astype(BF16)
    lse_ref[...] = jnp.concatenate(log_totals, axis=1)


def attend(normed_one, geo, w_attn, q_cols, kv_cols):
    group = normed_one.shape[0]
    both = q_cols + 2 * kv_cols
    qkv = jnp.dot(normed_one, w_attn[:, :both], preferred_element_type=F32)
    rotated, mixed, log_total = pl.pallas_call(
        attend_kernel,
        out_shape=(
            jax.ShapeDtypeStruct((group, both), BF16),
            jax.ShapeDtypeStruct((group, q_cols), BF16),
            jax.ShapeDtypeStruct((group, q_cols // HEAD), F32),
        ),
        compiler_params=pltpu.CompilerParams(vmem_limit_bytes=VMEM_BYTES),
    )(qkv, *geo)
    out_term = contract(mixed, w_attn[:, both : both + q_cols], 1, 1).astype(BF16)
    return (out_term, rotated, log_total, mixed)


def attend_back_kernel(d_mixed_ref, rot_ref, lse_ref, table_ref, bias_ref, out_ref):
    q_cols = d_mixed_ref.shape[1]
    cosine, sine_part = (table_ref[0], table_ref[1])
    keys, values = heads_of(rot_ref[:, q_cols:])
    bias = bias_ref[...]
    d_keys = [0.0, 0.0]
    d_values = [0.0, 0.0]
    for slab in range(q_cols // LANES):
        cols = slice(slab * LANES, (slab + 1) * LANES)
        query = rot_ref[:, cols]
        d_mixed = d_mixed_ref[:, cols]
        d_query = 0.0
        for odd in range(2):
            head = 2 * slab + odd
            scores = contract(query, keys[odd], 1, 1) * SCALE + bias
            probs = jnp.exp(scores - lse_ref[:, head : head + 1])
            d_probs = contract(d_mixed, values[odd], 1, 1)
            total = jnp.sum(d_probs * probs, axis=1, keepdims=True)
            d_scores = (probs * (d_probs - total)).astype(BF16)
            d_query = d_query + contract(d_scores, keys[odd], 1, 0)
            d_values[odd] = d_values[odd] + contract(probs.astype(BF16), d_mixed, 0, 0)
            d_keys[odd] = d_keys[odd] + contract(d_scores, query, 0, 0)
        d_query = d_query * SCALE
        out_ref[:, cols] = (d_query * cosine - half_swap(d_query) * sine_part).astype(BF16)
    low = lax.broadcasted_iota(jnp.int32, d_keys[0].shape, 1) < HEAD
    d_kv = jnp.where(
        low,
        (d_keys[0] + pltpu.roll(d_keys[1], HEAD, 1)) * SCALE,
        d_values[1] + pltpu.roll(d_values[0], HEAD, 1),
    )
    d_kv = d_kv * table_ref[2] - half_swap(d_kv) * table_ref[3]
    out_ref[:, q_cols:] = d_kv.astype(BF16)


def attend_back(grad_attn, geo, w_attn, at_first, rotated, log_total):
    other_attn = swap(core_half(grad_attn, at_first, False))
    both = rotated.shape[1]
    q_cols = log_total.shape[1] * HEAD
    w_out = w_attn[:, both : both + q_cols]
    d_mixed = jnp.dot(grad_attn, w_out, preferred_element_type=F32).astype(BF16)
    d_qkv = pl.pallas_call(
        attend_back_kernel,
        out_shape=jax.ShapeDtypeStruct(rotated.shape, BF16),
        compiler_params=pltpu.CompilerParams(vmem_limit_bytes=VMEM_BYTES),
    )(d_mixed, rotated, log_total, *geo)
    d_norm_one = contract(d_qkv, w_attn[:, :both], 1, 1).astype(BF16)
    return (d_qkv, swap(d_qkv), other_attn, d_norm_one)


def feed(normed_two, w_ffn, units):
    gate_up = jnp.dot(normed_two, w_ffn[:, : 2 * units], preferred_element_type=F32)
    hidden = (jax.nn.silu(gate_up[:, :units]) * gate_up[:, units:]).astype(BF16)
    return (gate_up, hidden)


def feed_back(grad_feed, gate_up, w_ffn):
    units = gate_up.shape[1] // 2
    d_hidden = jnp.dot(grad_feed, w_ffn[:, 2 * units :], preferred_element_type=F32)
    gate, up = (gate_up[:, :units], gate_up[:, units:])
    sigmoid_gate = jax.nn.sigmoid(gate)
    d_up = (d_hidden * gate * sigmoid_gate).astype(BF16)
    d_gate = (d_hidden * up * sigmoid_gate * (1.0 + gate * (1.0 - sigmoid_gate))).astype(BF16)
    d_gate_up = jnp.concatenate([d_gate, d_up], axis=1)
    other = swap(d_gate_up)
    return (d_gate_up, other, contract(d_gate_up, w_ffn[:, : 2 * units], 1, 1).astype(BF16))


def core_half(rows, at_first, own):
    width = rows.shape[1] // (2 * lax.axis_size("dp"))
    low, high = (
        jnp.concatenate(
            [rows[:, start : start + width] for start in range(first, rows.shape[1], 2 * width)],
            axis=1,
        )
        for first in (0, width)
    )
    return jnp.where(at_first, low, high) if own else jnp.where(at_first, high, low)


def exchange(at_first, rows, *whole):
    return tuple(swap(core_half(x, at_first, False)) for x in rows) + tuple(map(swap, whole))


def weight_grads_kernel(*refs):
    *pairs, out_ref = refs
    at = 0
    for k in range(0, len(pairs), 4):
        rows, other_rows, grads, other_grads = (ref[...] for ref in pairs[k : k + 4])
        total = contract(rows, grads, 0, 0) + contract(other_rows, other_grads, 0, 0)
        out_ref[:, at : at + total.shape[1]] = total.astype(BF16)
        at += total.shape[1]


def weight_grads(at_first, *pairs):
    pairs = [(core_half(rows, at_first, True), *rest) for rows, *rest in pairs]
    group, half = pairs[0][0].shape
    tile = min(256, half)
    specs = []
    for _, _, grads, _ in pairs:
        rows_spec = pl.BlockSpec((group, tile), lambda i: (0, i))
        grads_spec = pl.BlockSpec((group, grads.shape[1]), lambda i: (0, 0))
        specs += [rows_spec, rows_spec, grads_spec, grads_spec]
    total = sum(grads.shape[1] for _, _, grads, _ in pairs)
    return pl.pallas_call(
        weight_grads_kernel,
        grid=(half // tile,),
        in_specs=specs,
        out_specs=pl.BlockSpec((tile, total), lambda i: (i, 0)),
        out_shape=pltpu.HBM((half, total), BF16),
        compiler_params=pltpu.CompilerParams(vmem_limit_bytes=VMEM_BYTES),
    )(*[x for pair in pairs for x in pair])


def scatter(half):
    return lax.psum_scatter(half, "dp", scatter_dimension=0, tiled=True)


def norm_back(rows, inverse, gain, d_normed):
    unit = rows * inverse
    scaled = d_normed * gain
    return inverse * (scaled - unit * jnp.mean(scaled * unit, axis=1, keepdims=True))


def backward(
    kept, grad_all, grad, geo, weights, at_first, others, early, aside, down_job, last
):
    (layer_in, normed_one, rotated, log_total, mixed, middle, normed_two, gate_up, hidden) = kept
    norm_gain, ffn_gain, w_attn, w_ffn = weights
    run = aside.run if aside else lambda fn, *inputs: fn(*inputs)
    d_gate_up, other_gate_up, d_norm_two_all = run(feed_back, grad_all, gate_up, w_ffn)
    ffn_pair = (normed_two, others["normed_two"], d_gate_up, other_gate_up)
    down_pair = (grad_all, others["grad_all"], hidden, others["hidden"])
    d_norm_two_all, *ready = barrier(d_norm_two_all, *ffn_pair, *down_pair)
    ffn_pair, down_pair = (ready[:4], ready[4:])

    def grads(*given):
        pairs = [given[k : k + 4] for k in range(0, len(given), 4)]
        return (weight_grads(at_first, *pairs),)

    if last:
        jobs = (Job(grads, *ffn_pair, *down_pair), Job(lambda: (), held=early))
    else:
        jobs = (Job(grads, *ffn_pair), Job(grads, *down_pair, held=early))
    d_norm_two = collect(d_norm_two_all, jobs)
    early = jobs[1].held
    reduced = [scatter(job[0]) for job in jobs if job.results]
    d_middle = grad.astype(F32) + norm_back(middle, normalizer(middle), ffn_gain, d_norm_two)
    ffn_gain_job = Job(
        lambda d_all, normed: (
            jnp.sum(d_all.astype(F32) * (normed.astype(F32) / ffn_gain), axis=0),
        ),
        d_norm_two_all,
        normed_two,
    )
    grad_attn = spread(d_middle.astype(BF16), (ffn_gain_job, down_job))
    if down_job:
        aside = CollectRing(down_job[0])
    d_qkv, other_qkv, other_attn, d_norm_one_all = attend_back(
        grad_attn, geo, w_attn, at_first, rotated, log_total
    )
    pairs = (
        *(normed_one, others["normed_one"], d_qkv, other_qkv),
        *(grad_attn, other_attn, mixed, others["mixed"]),
    )
    d_norm_one_all, *pairs = barrier(d_norm_one_all, *pairs)
    attn_job = Job(grads, *pairs, held=reduced[:1] if last else ())
    attn_gain_job = Job(
        lambda d_all, normed: (
            jnp.sum(d_all.astype(F32) * (normed.astype(F32) / norm_gain), axis=0),
        ),
        d_norm_one_all,
        normed_one,
    )
    ffn_done = Job(lambda: (), held=() if last else reduced[:1])
    d_norm_one = collect(d_norm_one_all, (attn_job, attn_gain_job, ffn_done))
    reduced[:1] = attn_job.held or ffn_done.held
    g_attn = attn_job[0]
    d_input = d_middle + norm_back(layer_in, normalizer(layer_in), norm_gain, d_norm_one)
    gain_grads = jnp.stack([attn_gain_job[0], ffn_gain_job[0]])
    return (d_input.astype(BF16), (scatter(g_attn), *reduced), gain_grads, early, aside)


def both_layers(own, at_first):
    rows = own.shape[0] // 2
    low, high = (own[:rows], own[rows:])
    mine = jnp.where(at_first, low, high)
    got = swap(jnp.where(at_first, high, low))
    return (jnp.where(at_first, mine, got), jnp.where(at_first, got, mine))


def own_layer(first, second, at_first):
    mine = jnp.where(at_first, first, second)
    got = swap(jnp.where(at_first, second, first))
    return jnp.concatenate([jnp.where(at_first, mine, got), jnp.where(at_first, got, mine)], axis=0)


def gather(shard):
    return lax.all_gather(shard, ("dp", "section"), axis=0, tiled=True)


def reduce_small(rows):
    for axis in ("tensor", "dp"):
        count = lax.axis_size(axis)
        if axis == "tensor":
            parts = rows.reshape(rows.shape[0], lax.axis_size("dp"), count, -1).transpose(2, 0, 1, 3)
        else:
            parts = rows.transpose(1, 0, 2)
        me = lax.axis_index(axis)
        rows = lax.dynamic_index_in_dim(parts, me, 0, keepdims=False)
        for k in range(1, count):
            part = lax.dynamic_index_in_dim(parts, (me + k) % count, 0, keepdims=False)
            rows = rows + turn(part, axis, k)
    return rows + swap(rows)


def local(
    tokens_in,
    cotangent,
    lengths,
    attn_gain,
    w_query,
    w_key,
    w_value,
    w_out,
    ffn_gain,
    w_gate,
    w_up,
    w_down,
):
    at_first = lax.axis_index("section") == 0
    rows = tokens_in.shape[1]
    q_cols, kv_cols, units = (w_query.shape[2], w_key.shape[2], w_gate.shape[2])
    tokens = jnp.where(at_first, tokens_in[0], tokens_in[1])
    upstream = jnp.where(at_first, cotangent[0], cotangent[1])
    gains_cols = jnp.pad(
        jnp.concatenate([attn_gain, ffn_gain], axis=0).T, ((0, 0), (0, LANES - 2))
    )
    attn_rows = jnp.concatenate(
        [w_query[0], w_key[0], w_value[0], w_out[0].T, gains_cols], axis=1
    )
    attn_rows, tokens = barrier(attn_rows, tokens)
    attn_parts = both_layers(attn_rows, at_first)
    prepare = Job(
        lambda gate, up, down: both_layers(
            jnp.concatenate([gate, up, down.T], axis=1), at_first
        ),
        w_gate[0],
        w_up[0],
        w_down[0],
    )
    tokens_all = spread(tokens, (prepare,))
    first_attn = gather(attn_parts[0])
    first_ffn = gather(prepare[0])
    w_attns = [first_attn, gather(attn_parts[1])]
    w_ffns = [first_ffn, gather(prepare[1])]
    geo = geometry(jnp.where(at_first, lengths[0, 0], lengths[1, 0]), rows)
    tokens_all = tokens_all.astype(F32)
    layer_in = tokens.astype(F32)
    layers = []
    for layer in range(2):
        w_attn, w_ffn = (w_attns[layer], w_ffns[layer])
        norm_gain, ffn_gain = (
            w_attn[:, 2 * (q_cols + kv_cols) :][:, :2].T.astype(F32)
        )
        if layer:
            normed_one = spread((layer_in * normalizer(layer_in) * norm_gain).astype(BF16))
        else:
            normed_one = (tokens_all * normalizer(tokens_all) * norm_gain).astype(BF16)
        out_term, rotated, log_total, mixed = attend(normed_one, geo, w_attn, q_cols, kv_cols)
        attn_swap = Job(lambda one, heads: exchange(at_first, (one,), heads), normed_one, mixed)
        others = {}
        grad_swap = None
        if layer:
            grad_swap = Job(lambda x: exchange(at_first, (x,)), upstream_all)
        middle = layer_in + collect(out_term, (None, attn_swap, grad_swap))
        others.update(normed_one=attn_swap[0], mixed=attn_swap[1])
        if layer:
            others.update(grad_all=grad_swap[0])
        normed_two = spread((middle * normalizer(middle) * ffn_gain).astype(BF16))
        if layer:
            gate_up, hidden = feed(normed_two, w_ffn, units)
        else:
            normed_two, upstream = barrier(normed_two, upstream)
            upstream_ring = SpreadRing(upstream)
            upstream_ring.run(lambda: ())
            upstream_ring.run(lambda: ())
            gate_up, hidden = upstream_ring.run(
                lambda normed, w: feed(normed, w, units), normed_two, w_ffn
            )
            upstream_all = upstream_ring.finish()
        down_job = Job(
            lambda hidden, w: (contract(hidden, w[:, 2 * units :], 1, 1).astype(BF16),),
            hidden,
            w_ffn,
        )
        if layer == 0:
            (down_term,) = down_job.fn(*down_job.inputs)
            ffn_swap = Job(
                lambda two, units: exchange(at_first, (two,), units), normed_two, hidden
            )
            first_out = (middle + collect(down_term, (None, ffn_swap))).astype(BF16)
            others.update(normed_two=ffn_swap[0], hidden=ffn_swap[1])
        else:
            others.update(
                zip(("normed_two", "hidden"), exchange(at_first, (normed_two,), hidden))
            )
        kept = (
            layer_in, normed_one, rotated, log_total, mixed, middle, normed_two, gate_up, hidden
        )
        layers.append((kept, (norm_gain, ffn_gain, w_attn, w_ffn), others))
        layer_in = first_out.astype(F32)

    def back(layer, grad_all, grad, early, aside, down_job):
        kept, weights, others = layers[layer]
        if "grad_all" not in others:
            others["grad_all"] = exchange(at_first, (grad_all,))[0]
        return backward(
            kept,
            grad_all,
            grad,
            geo,
            weights,
            at_first,
            others,
            early,
            aside,
            down_job,
            layer == 0,
        )

    d_second, (second_attn, second_ffn, second_down), second_gains, _, out_ring = back(
        1, upstream_all, upstream, (), None, down_job
    )
    down_done = Job(lambda: (), held=(second_down,))
    d_second_all = spread(d_second, (None, down_done))
    d_first, (first_attn, first_ffn), first_gains, (second_attn,), _ = back(
        0, d_second_all, d_second, (second_attn,), out_ring, None
    )
    second_out = (middle + out_ring.finish()).astype(BF16)
    second_ffn = jnp.concatenate([second_ffn, *down_done.held], axis=1)
    g_gains = reduce_small(jnp.concatenate([first_gains, second_gains]))
    gain_own = jnp.where(at_first, g_gains[:2], g_gains[2:])

    def by_layer(first, second):
        mine = jnp.where(at_first, first, second)
        got = swap(jnp.where(at_first, second, first))
        return jnp.stack([jnp.where(at_first, mine, got), jnp.where(at_first, got, mine)])

    section_out = by_layer(first_out, second_out)
    input_grad = by_layer(d_first, d_second)
    g_ffn = own_layer(first_ffn, second_ffn, at_first).astype(F32)
    g_gate, g_up, g_down = (
        g_ffn[:, :units], g_ffn[:, units : 2 * units], g_ffn[:, 2 * units :].T
    )
    first_attn, gain_own, section_out, input_grad, g_gate, g_up, g_down = barrier(
        first_attn, gain_own, section_out, input_grad, g_gate, g_up, g_down
    )
    g_attn = own_layer(first_attn, second_attn, at_first).astype(F32)
    qkv = q_cols + 2 * kv_cols
    return (
        section_out[None],
        input_grad[None],
        gain_own[0][None],
        g_attn[:, :q_cols][None],
        g_attn[:, q_cols : q_cols + kv_cols][None],
        g_attn[:, q_cols + kv_cols : qkv][None],
        g_attn[:, qkv:].T[None],
        gain_own[1][None],
        g_gate[None],
        g_up[None],
        g_down[None],
    )


def solution(mesh):
    return jax.shard_map(
        local,
        mesh=mesh,
        in_specs=(
            P(None, ("dp", "tensor"), None),
            P(None, ("dp", "tensor"), None),
            P(None, "dp", None),
            P("section", "dp"),
            P("section", "dp", "tensor"),
            P("section", "dp", "tensor"),
            P("section", "dp", "tensor"),
            P("section", "tensor", "dp"),
            P("section", "dp"),
            P("section", "dp", "tensor"),
            P("section", "dp", "tensor"),
            P("section", "tensor", "dp"),
        ),
        out_specs=(
            P("section", None, ("dp", "tensor"), None),
            P("section", None, ("dp", "tensor"), None),
            P("section", ("dp", "tensor")),
            P("section", "dp", "tensor"),
            P("section", "dp", "tensor"),
            P("section", "dp", "tensor"),
            P("section", "tensor", "dp"),
            P("section", ("dp", "tensor")),
            P("section", "dp", "tensor"),
            P("section", "dp", "tensor"),
            P("section", "tensor", "dp"),
        ),
        check_vma=False,
    )
```

```python
import jax
import jax.numpy as jnp
from jax import lax
from jax.experimental import pallas as pl
from jax.experimental.pallas import tpu as pltpu
from jax.sharding import PartitionSpec as P

HEAD = 64


EPSILON = 1e-05
MASK_FILL = -1e30
BF16 = jnp.bfloat16
F32 = jnp.float32
LANES = 128
SCALE = HEAD ** (-0.5)
VMEM_BYTES = 12 * 2**20
GRADS_VMEM_BYTES = 20 * 2**20


def turn(value, axis, steps):
    count = lax.axis_size(axis)
    return lax.ppermute(value, axis, [(i, (i + steps) % count) for i in range(count)])


def swap(value):
    return lax.ppermute(value, "section", [(0, 1), (1, 0)])


def contract(left, right, left_dim, right_dim):
    return lax.dot_general(
        left, right, (((left_dim,), (right_dim,)), ((), ())), preferred_element_type=F32
    )


def geometry(seq_lens, rows):
    count = lax.axis_size("tensor")
    place = (lax.axis_index("tensor") - jnp.arange(count, dtype=jnp.int32)) % count
    row_ids = (place[:, None] * rows + jnp.arange(rows, dtype=jnp.int32)[None, :]).reshape(-1)
    ends = jnp.cumsum(seq_lens)
    starts = ends - seq_lens
    member = jnp.sum((row_ids[:, None] >= ends[None, :]).astype(jnp.int32), axis=1)
    slots = jnp.arange(seq_lens.shape[0], dtype=jnp.int32)
    begins = jnp.sum(jnp.where(member[:, None] == slots[None, :], starts[None, :], 0), axis=1)
    position = row_ids - begins
    half_dim = HEAD // 2
    frequency = 10000.0 ** (-jnp.arange(half_dim, dtype=F32) / half_dim)
    angle = position.astype(F32)[:, None] * frequency[None, :]
    allowed = (member[:, None] == member[None, :]) & (row_ids[:, None] >= row_ids[None, :])
    cosine, sine_part = (jnp.cos(angle), jnp.sin(angle))
    cosine = jnp.concatenate([cosine] * (LANES // half_dim), axis=1)
    sine_part = jnp.concatenate([-sine_part, sine_part] * (LANES // HEAD), axis=1)
    turned = jnp.arange(LANES) < HEAD
    tables = jnp.stack(
        [cosine, sine_part, jnp.where(turned, cosine, 1.0), jnp.where(turned, sine_part, 0.0)]
    )
    return (tables, jnp.where(allowed, 0.0, MASK_FILL))


def barrier(*values):
    return lax.optimization_barrier(values)


class Job:
    def __init__(self, fn, *inputs, held=()):
        self.fn, self.inputs, self.held, self.results = (fn, inputs, held, None)

    def __getitem__(self, which):
        return self.results[which]


def step(value, job):
    if job is None:
        return turn(value, "tensor", 1)
    inputs = job.inputs() if callable(job.inputs) else job.inputs
    value, *inputs = barrier(value, *inputs)
    results = job.fn(*inputs)
    recv, *values = barrier(turn(value, "tensor", 1), *results, *job.held)
    job.results, job.held = (values[: len(results)], values[len(results) :])
    return recv


def spread(block, jobs=()):
    pieces = [block]
    for k in range(lax.axis_size("tensor") - 1):
        pieces.append(step(pieces[-1], jobs[k] if k < len(jobs) else None))
    return jnp.concatenate(pieces, axis=0)


def collect(partial, jobs=()):
    count = lax.axis_size("tensor")
    rows = partial.shape[0] // count
    blocks = partial.reshape(count, rows, partial.shape[1])
    total = blocks[1 % count]
    for k in range(count - 1):
        recv = step(total.astype(BF16), jobs[k] if k < len(jobs) else None)
        total = recv.astype(F32) + blocks[(k + 2) % count].astype(F32)
    return total


class Ring:
    def __init__(self, first):
        self.count, self.taken, self.value = (lax.axis_size("tensor"), 0, first)

    def run(self, fn, *inputs):
        if self.taken == self.count - 1:
            return fn(*inputs)
        job = Job(fn, *inputs)
        self.accept(step(self.value, job))
        self.taken += 1
        return tuple(job.results)

    def finish(self):
        while self.taken < self.count - 1:
            self.run(lambda: ())
        return self.result()


class SpreadRing(Ring):
    def __init__(self, block):
        super().__init__(block)
        self.pieces = [block]

    def accept(self, recv):
        self.pieces.append(recv)
        self.value = recv

    def result(self):
        return jnp.concatenate(self.pieces, axis=0)


class CollectRing(Ring):
    def __init__(self, partial):
        count = lax.axis_size("tensor")
        self.blocks = partial.reshape(count, partial.shape[0] // count, partial.shape[1])
        self.total = self.blocks[1 % count].astype(F32)
        super().__init__(self.total.astype(BF16))

    def accept(self, recv):
        block = self.blocks[(self.taken + 2) % self.count]
        self.total = recv.astype(F32) + block.astype(F32)
        self.value = self.total.astype(BF16)

    def result(self):
        return self.total


def estimate(us):
    return pl.CostEstimate(flops=0, bytes_accessed=int(us * 3.3e6), transcendentals=0)


def normalizer(rows):
    return lax.rsqrt(jnp.mean(rows * rows, axis=1, keepdims=True) + EPSILON)


def half_swap(x):
    lane = lax.broadcasted_iota(jnp.int32, x.shape, 1)
    first = (lane % HEAD) < HEAD // 2
    return jnp.where(
        first, pltpu.roll(x, LANES - HEAD // 2, 1), pltpu.roll(x, HEAD // 2, 1)
    )


def heads_of(kv):
    low = lax.broadcasted_iota(jnp.int32, kv.shape, 1) < HEAD
    kv = kv.astype(F32)
    turned = pltpu.roll(kv, HEAD, 1)
    keys = (jnp.where(low, kv, 0.0).astype(BF16), jnp.where(low, 0.0, turned).astype(BF16))
    values = (jnp.where(low, turned, 0.0).astype(BF16), jnp.where(low, 0.0, kv).astype(BF16))
    return (keys, values)


def attend_kernel(qkv_ref, table_ref, bias_ref, rot_ref, mixed_ref, lse_ref):
    q_cols = mixed_ref.shape[1]
    cosine, sine_part = (table_ref[0], table_ref[1])
    kv = qkv_ref[:, q_cols:]
    kv = (kv * table_ref[2] + half_swap(kv) * table_ref[3]).astype(BF16)
    rot_ref[:, q_cols:] = kv
    keys, values = heads_of(kv)
    bias = bias_ref[...]
    head_ids = lax.broadcasted_iota(jnp.int32, lse_ref.shape, 1)

    def one_slab(slab, log_totals):
        cols = pl.ds(pl.multiple_of(slab * LANES, LANES), LANES)
        query = qkv_ref[:, cols]
        query = (query * cosine + half_swap(query) * sine_part).astype(BF16)
        rot_ref[:, cols] = query
        mixed = 0.0
        for odd in range(2):
            scores = contract(query, keys[odd], 1, 1) * SCALE + bias
            row_max = jnp.max(scores, axis=1, keepdims=True)
            exponent = jnp.exp(scores - row_max)
            totals = jnp.sum(exponent, axis=1, keepdims=True)
            log_total = row_max + jnp.log(totals)
            log_totals = jnp.where(head_ids == 2 * slab + odd, log_total, log_totals)
            mixed = mixed + contract((exponent / totals).astype(BF16), values[odd], 1, 0)
        mixed_ref[:, cols] = mixed.astype(BF16)
        return log_totals

    lse_ref[...] = lax.fori_loop(
        0, q_cols // LANES, one_slab, jnp.zeros(lse_ref.shape, F32)
    )


def attend(normed_one, geo, w_attn, q_cols, kv_cols):
    group = normed_one.shape[0]
    both = q_cols + 2 * kv_cols
    qkv = jnp.dot(normed_one, w_attn[:, :both], preferred_element_type=F32)
    rotated, mixed, log_total = pl.pallas_call(
        attend_kernel,
        out_shape=(
            jax.ShapeDtypeStruct((group, both), BF16),
            jax.ShapeDtypeStruct((group, q_cols), BF16),
            jax.ShapeDtypeStruct((group, q_cols // HEAD), F32),
        ),
        cost_estimate=estimate(3),
        compiler_params=pltpu.CompilerParams(vmem_limit_bytes=VMEM_BYTES),
    )(qkv, *geo)
    out_term = contract(mixed, w_attn[:, both : both + q_cols], 1, 1).astype(BF16)
    return (out_term, rotated, log_total, mixed)


def attend_back_kernel(d_mixed_ref, rot_ref, lse_ref, table_ref, bias_ref, out_ref):
    q_cols = d_mixed_ref.shape[1]
    cosine, sine_part = (table_ref[0], table_ref[1])
    keys, values = heads_of(rot_ref[:, q_cols:])
    bias = bias_ref[...]
    log_totals = lse_ref[...]
    head_ids = lax.broadcasted_iota(jnp.int32, log_totals.shape, 1)

    def one_slab(slab, sums):
        d_keys, d_values = (list(sums[:2]), list(sums[2:]))
        cols = pl.ds(pl.multiple_of(slab * LANES, LANES), LANES)
        query = rot_ref[:, cols]
        d_mixed = d_mixed_ref[:, cols]
        d_query = 0.0
        for odd in range(2):
            log_total = jnp.sum(
                jnp.where(head_ids == 2 * slab + odd, log_totals, 0.0), axis=1, keepdims=True
            )
            scores = contract(query, keys[odd], 1, 1) * SCALE + bias
            probs = jnp.exp(scores - log_total)
            d_probs = contract(d_mixed, values[odd], 1, 1)
            total = jnp.sum(d_probs * probs, axis=1, keepdims=True)
            d_scores = (probs * (d_probs - total)).astype(BF16)
            d_query = d_query + contract(d_scores, keys[odd], 1, 0)
            d_values[odd] = d_values[odd] + contract(probs.astype(BF16), d_mixed, 0, 0)
            d_keys[odd] = d_keys[odd] + contract(d_scores, query, 0, 0)
        d_query = d_query * SCALE
        out_ref[:, cols] = (d_query * cosine - half_swap(d_query) * sine_part).astype(BF16)
        return (*d_keys, *d_values)

    zeros = jnp.zeros((d_mixed_ref.shape[0], LANES), F32)
    sums = lax.fori_loop(0, q_cols // LANES, one_slab, (zeros,) * 4)
    d_keys, d_values = (sums[:2], sums[2:])
    low = lax.broadcasted_iota(jnp.int32, d_keys[0].shape, 1) < HEAD
    d_kv = jnp.where(
        low,
        (d_keys[0] + pltpu.roll(d_keys[1], HEAD, 1)) * SCALE,
        d_values[1] + pltpu.roll(d_values[0], HEAD, 1),
    )
    d_kv = d_kv * table_ref[2] - half_swap(d_kv) * table_ref[3]
    out_ref[:, q_cols:] = d_kv.astype(BF16)


def attend_back(grad_attn, geo, w_attn, at_first, rotated, log_total):
    other_attn = swap(core_half(grad_attn, at_first, False))
    both = rotated.shape[1]
    q_cols = log_total.shape[1] * HEAD
    w_out = w_attn[:, both : both + q_cols]
    d_mixed = jnp.dot(grad_attn, w_out, preferred_element_type=F32).astype(BF16)
    d_qkv = pl.pallas_call(
        attend_back_kernel,
        out_shape=jax.ShapeDtypeStruct(rotated.shape, BF16),
        cost_estimate=estimate(6),
        compiler_params=pltpu.CompilerParams(vmem_limit_bytes=VMEM_BYTES),
    )(d_mixed, rotated, log_total, *geo)
    d_norm_one = contract(d_qkv, w_attn[:, :both], 1, 1).astype(BF16)
    return (d_qkv, swap(d_qkv), other_attn, d_norm_one)


def feed(normed_two, w_ffn, units):
    gate_up = jnp.dot(normed_two, w_ffn[:, : 2 * units], preferred_element_type=F32)
    hidden = (jax.nn.silu(gate_up[:, :units]) * gate_up[:, units:]).astype(BF16)
    return (gate_up, hidden)


def feed_back(grad_feed, gate_up, w_ffn):
    units = gate_up.shape[1] // 2
    d_hidden = jnp.dot(grad_feed, w_ffn[:, 2 * units :], preferred_element_type=F32)
    gate, up = (gate_up[:, :units], gate_up[:, units:])
    sigmoid_gate = jax.nn.sigmoid(gate)
    d_up = (d_hidden * gate * sigmoid_gate).astype(BF16)
    d_gate = (d_hidden * up * sigmoid_gate * (1.0 + gate * (1.0 - sigmoid_gate))).astype(BF16)
    return (jnp.concatenate([d_gate, d_up], axis=1),)


def feed_back_rows(d_gate_up, w_ffn):
    return (contract(d_gate_up, w_ffn[:, : d_gate_up.shape[1]], 1, 1).astype(BF16),)


def core_half(rows, at_first, own):
    width = rows.shape[1] // (2 * lax.axis_size("dp"))
    low, high = (
        jnp.concatenate(
            [rows[:, start : start + width] for start in range(first, rows.shape[1], 2 * width)],
            axis=1,
        )
        for first in (0, width)
    )
    return jnp.where(at_first, low, high) if own else jnp.where(at_first, high, low)


def exchange(at_first, rows, *whole):
    return tuple(swap(core_half(x, at_first, False)) for x in rows) + tuple(map(swap, whole))


def weight_grads_kernel(_, *refs):
    *pairs, out_ref = refs
    at = 0
    for k in range(0, len(pairs), 4):
        rows, other_rows, grads, other_grads = (ref[...] for ref in pairs[k : k + 4])
        total = contract(rows, grads, 0, 0) + contract(other_rows, other_grads, 0, 0)
        out_ref[:, at : at + total.shape[1]] = total.astype(BF16)
        at += total.shape[1]


def weight_grads(at_first, *pairs):
    group, half = pairs[0][1].shape
    n_dp = lax.axis_size("dp")
    tile = half // n_dp
    direct = tile % LANES == 0
    if not direct:
        pairs = [(core_half(rows, at_first, True), *rest) for rows, *rest in pairs]
        tile = min(256, half)
    specs = []
    for _, _, grads, _ in pairs:
        own_spec = pl.BlockSpec((group, tile), lambda i, core: (0, 2 * i + core[0]))
        half_spec = pl.BlockSpec((group, tile), lambda i, core: (0, i))
        grads_spec = pl.BlockSpec(
            (group, grads.shape[1]), lambda i, core: (0, 0), pipeline_mode=pl.Buffered(1)
        )
        specs += [own_spec if direct else half_spec, half_spec, grads_spec, grads_spec]
    total = sum(grads.shape[1] for _, _, grads, _ in pairs)
    return pl.pallas_call(
        weight_grads_kernel,
        grid_spec=pltpu.PrefetchScalarGridSpec(
            num_scalar_prefetch=1,
            grid=(half // tile,),
            in_specs=specs,
            out_specs=pl.BlockSpec((tile, total), lambda i, core: (i, 0)),
        ),
        out_shape=pltpu.HBM((half, total), BF16),
        cost_estimate=estimate(total / 330),
        compiler_params=pltpu.CompilerParams(vmem_limit_bytes=GRADS_VMEM_BYTES),
    )(
        jnp.where(at_first, 0, 1).astype(jnp.int32).reshape(1),
        *[x for pair in pairs for x in pair],
    )


def scatter(half):
    return lax.psum_scatter(half, "dp", scatter_dimension=0, tiled=True)


def norm_back(rows, inverse, gain, d_normed):
    unit = rows * inverse
    scaled = d_normed * gain
    return inverse * (scaled - unit * jnp.mean(scaled * unit, axis=1, keepdims=True))


def backward(
    kept, grad_all, grad, geo, weights, at_first, others, early, aside, down_job
):
    (layer_in, normed_one, rotated, log_total, mixed, middle, normed_two, gate_up, hidden) = kept
    norm_gain, ffn_gain, w_attn, w_ffn = weights
    last = down_job is None
    run = aside.run if aside else lambda fn, *inputs: fn(*inputs)
    (d_gate_up,) = run(feed_back, grad_all, gate_up, w_ffn)
    (d_norm_two_all,) = run(feed_back_rows, d_gate_up, w_ffn)
    if last:
        d_gate_up, grad_all = barrier(d_gate_up, grad_all)
        others["grad_all"] = exchange(at_first, (grad_all,))[0]

    def grads(*given):
        pairs = [given[k : k + 4] for k in range(0, len(given), 4)]
        return (weight_grads(at_first, *pairs),)

    if last:
        pairs = (
            *(normed_two, others["normed_two"], d_gate_up, swap(d_gate_up)),
            *(grad_all, others["grad_all"], hidden, others["hidden"]),
        )
        d_norm_two_all, *pairs = barrier(d_norm_two_all, *pairs)
        grads_jobs = (Job(grads, *pairs), Job(lambda: (), held=early))
        d_norm_two = collect(d_norm_two_all, grads_jobs)
        early = grads_jobs[1].held
    else:
        swap_job = Job(
            lambda d_gate_up, hidden, *rows: (
                swap(d_gate_up), swap(hidden), *exchange(at_first, rows)
            ),
            d_gate_up,
            hidden,
            normed_two,
            grad_all,
        )
        grads_jobs = (Job(grads), Job(grads))
        grads_jobs[0].inputs = lambda: (normed_two, swap_job[2], d_gate_up, swap_job[0])
        grads_jobs[1].inputs = lambda: (grad_all, swap_job[3], hidden, swap_job[1])
        d_norm_two = collect(d_norm_two_all, (swap_job, *grads_jobs))
    reduced = [scatter(job[0]) for job in grads_jobs if job.results]
    d_middle = grad.astype(F32) + norm_back(middle, normalizer(middle), ffn_gain, d_norm_two)
    ffn_gain_job = Job(
        lambda d_all, normed: (
            jnp.sum(d_all.astype(F32) * (normed.astype(F32) / ffn_gain), axis=0),
        ),
        d_norm_two_all,
        normed_two,
    )
    if last:
        aside_job = Job(lambda value: (turn(value, "tensor", 1),), aside.value)
        grad_attn = spread(d_middle.astype(BF16), (ffn_gain_job, aside_job))
        aside.accept(aside_job[0])
        aside.taken += 1
    else:
        grad_attn = spread(d_middle.astype(BF16), (ffn_gain_job, down_job))
        aside = CollectRing(down_job[0])
    d_qkv, other_qkv, other_attn, d_norm_one_all = attend_back(
        grad_attn, geo, w_attn, at_first, rotated, log_total
    )
    other_one, other_mixed = others.get("attn") or exchange(at_first, (normed_one,), mixed)
    pairs = (
        *(normed_one, other_one, d_qkv, other_qkv),
        *(grad_attn, other_attn, mixed, other_mixed),
    )
    d_norm_one_all, *pairs = barrier(d_norm_one_all, *pairs)
    attn_job = Job(grads, *pairs, held=reduced[:1] if last else ())
    attn_gain_job = Job(
        lambda d_all, normed: (
            jnp.sum(d_all.astype(F32) * (normed.astype(F32) / norm_gain), axis=0),
        ),
        d_norm_one_all,
        normed_one,
    )
    last_job = Job(lambda: (), held=() if last else reduced[:1])
    d_norm_one = collect(d_norm_one_all, (attn_job, attn_gain_job, last_job))
    reduced[:1] = attn_job.held or last_job.held
    g_attn = attn_job[0]
    d_input = d_middle + norm_back(layer_in, normalizer(layer_in), norm_gain, d_norm_one)
    gain_grads = jnp.stack([attn_gain_job[0], ffn_gain_job[0]])
    return (d_input.astype(BF16), (scatter(g_attn), *reduced), gain_grads, early, aside)


def both_layers(own, at_first):
    rows = own.shape[0] // 2
    low, high = (own[:rows], own[rows:])
    mine = jnp.where(at_first, low, high)
    got = swap(jnp.where(at_first, high, low))
    return (jnp.where(at_first, mine, got), jnp.where(at_first, got, mine))


def own_layer(first, second, at_first):
    mine = jnp.where(at_first, first, second)
    got = swap(jnp.where(at_first, second, first))
    return jnp.concatenate([jnp.where(at_first, mine, got), jnp.where(at_first, got, mine)], axis=0)


def gather(shard):
    return lax.all_gather(shard, ("dp", "section"), axis=0, tiled=True)


def reduce_small(rows):
    for axis in ("tensor", "dp"):
        count = lax.axis_size(axis)
        if axis == "tensor":
            parts = rows.reshape(rows.shape[0], lax.axis_size("dp"), count, -1).transpose(2, 0, 1, 3)
        else:
            parts = rows.transpose(1, 0, 2)
        me = lax.axis_index(axis)
        rows = lax.dynamic_index_in_dim(parts, me, 0, keepdims=False)
        for k in range(1, count):
            part = lax.dynamic_index_in_dim(parts, (me + k) % count, 0, keepdims=False)
            rows = rows + turn(part, axis, k)
    return rows + swap(rows)


def local(
    tokens_in,
    cotangent,
    lengths,
    attn_gain,
    w_query,
    w_key,
    w_value,
    w_out,
    ffn_gain,
    w_gate,
    w_up,
    w_down,
):
    at_first = lax.axis_index("section") == 0
    rows = tokens_in.shape[1]
    q_cols, kv_cols, units = (w_query.shape[2], w_key.shape[2], w_gate.shape[2])
    tokens = jnp.where(at_first, tokens_in[0], tokens_in[1])
    upstream = jnp.where(at_first, cotangent[0], cotangent[1])
    gains_cols = jnp.pad(
        jnp.concatenate([attn_gain, ffn_gain], axis=0).T, ((0, 0), (0, LANES - 2))
    )
    attn_rows = jnp.concatenate(
        [w_query[0], w_key[0], w_value[0], w_out[0].T, gains_cols], axis=1
    )
    attn_rows, tokens = barrier(attn_rows, tokens)
    attn_parts = both_layers(attn_rows, at_first)
    prepare = Job(
        lambda gate, up, down: both_layers(
            jnp.concatenate([gate, up, down.T], axis=1), at_first
        ),
        w_gate[0],
        w_up[0],
        w_down[0],
    )
    tokens_all = spread(tokens, (None, prepare))
    tokens_all, upstream = barrier(tokens_all, upstream)
    upstream_ring = SpreadRing(upstream)
    first_attn = gather(attn_parts[0])
    first_ffn = gather(prepare[0])
    w_attns = [first_attn, gather(attn_parts[1])]
    w_ffns = [first_ffn]
    geo = geometry(jnp.where(at_first, lengths[0, 0], lengths[1, 0]), rows)
    tokens_all = tokens_all.astype(F32)
    layer_in = tokens.astype(F32)
    layers = []
    for layer in range(2):
        w_attn, w_ffn = (w_attns[layer], w_ffns[layer])
        norm_gain, ffn_gain = (
            w_attn[:, 2 * (q_cols + kv_cols) :][:, :2].T.astype(F32)
        )
        if layer:
            normed_one = spread((layer_in * normalizer(layer_in) * norm_gain).astype(BF16))
        else:
            normed_one = (tokens_all * normalizer(tokens_all) * norm_gain).astype(BF16)
        attention = (lambda normed, w: attend(normed, geo, w, q_cols, kv_cols), normed_one, w_attn)
        out_term, rotated, log_total, mixed = upstream_ring.run(*attention)
        middle = layer_in + collect(out_term)
        normed_two = spread((middle * normalizer(middle) * ffn_gain).astype(BF16))
        others = {}
        if layer == 0:
            normed_two, upstream_ring.value = barrier(normed_two, upstream_ring.value)
            others.update(
                attn=upstream_ring.run(
                    lambda one, heads: exchange(at_first, (one,), heads), normed_one, mixed
                )
            )
            normed_two, upstream_ring.value = barrier(normed_two, upstream_ring.value)
        gate_up, hidden = feed(normed_two, w_ffn, units)
        down_job = Job(
            lambda hidden, w: (contract(hidden, w[:, 2 * units :], 1, 1).astype(BF16),),
            hidden,
            w_ffn,
        )
        if layer == 0:
            (down_term,) = down_job.fn(*down_job.inputs)
            ffn_swap = Job(
                lambda two, units: exchange(at_first, (two,), units), normed_two, hidden
            )
            first_out = (middle + collect(down_term, (None, ffn_swap))).astype(BF16)
            others.update(normed_two=ffn_swap[0], hidden=ffn_swap[1])
            first_out, ffn_part = barrier(first_out, prepare[1])
            w_ffns.append(gather(ffn_part))
        kept = (
            layer_in, normed_one, rotated, log_total, mixed, middle, normed_two, gate_up, hidden
        )
        layers.append((kept, (norm_gain, ffn_gain, w_attn, w_ffn), others))
        layer_in = first_out.astype(F32)

    def back(layer, grad_all, grad, early, aside, down_job):
        kept, weights, others = layers[layer]
        return backward(
            kept,
            grad_all,
            grad,
            geo,
            weights,
            at_first,
            others,
            early,
            aside,
            down_job,
        )

    upstream_all = upstream_ring.finish()
    d_second, (second_attn, second_ffn, second_down), second_gains, _, out_ring = back(
        1, upstream_all, upstream, (), None, down_job
    )
    down_done = Job(lambda: (), held=(second_down,))
    d_second_all = spread(d_second, (None, down_done))
    d_first, (first_attn, first_ffn), first_gains, (second_attn,), _ = back(
        0, d_second_all, d_second, (second_attn,), out_ring, None
    )
    second_out = (middle + out_ring.finish()).astype(BF16)
    second_ffn = jnp.concatenate([second_ffn, *down_done.held], axis=1)
    g_gains = reduce_small(jnp.concatenate([first_gains, second_gains]))
    gain_own = jnp.where(at_first, g_gains[:2], g_gains[2:])

    def by_layer(first, second):
        mine = jnp.where(at_first, first, second)
        got = swap(jnp.where(at_first, second, first))
        return jnp.stack([jnp.where(at_first, mine, got), jnp.where(at_first, got, mine)])

    section_out = by_layer(first_out, second_out)
    input_grad = by_layer(d_first, d_second)
    g_ffn = own_layer(first_ffn, second_ffn, at_first).astype(F32)
    g_gate, g_up, g_down = (
        g_ffn[:, :units], g_ffn[:, units : 2 * units], g_ffn[:, 2 * units :].T
    )
    first_attn, gain_own, section_out, input_grad, g_gate, g_up, g_down = barrier(
        first_attn, gain_own, section_out, input_grad, g_gate, g_up, g_down
    )
    g_attn = own_layer(first_attn, second_attn, at_first).astype(F32)
    qkv = q_cols + 2 * kv_cols
    g_key_value = g_attn[:, q_cols:qkv].T
    return (
        section_out[None],
        input_grad[None],
        gain_own[0][None],
        g_attn[:, :q_cols][None],
        g_key_value[:kv_cols].T[None],
        g_key_value[kv_cols:].T[None],
        g_attn[:, qkv:].T[None],
        gain_own[1][None],
        g_gate[None],
        g_up[None],
        g_down[None],
    )


def solution(mesh):
    return jax.shard_map(
        local,
        mesh=mesh,
        in_specs=(
            P(None, ("dp", "tensor"), None),
            P(None, ("dp", "tensor"), None),
            P(None, "dp", None),
            P("section", "dp"),
            P("section", "dp", "tensor"),
            P("section", "dp", "tensor"),
            P("section", "dp", "tensor"),
            P("section", "tensor", "dp"),
            P("section", "dp"),
            P("section", "dp", "tensor"),
            P("section", "dp", "tensor"),
            P("section", "tensor", "dp"),
        ),
        out_specs=(
            P("section", None, ("dp", "tensor"), None),
            P("section", None, ("dp", "tensor"), None),
            P("section", ("dp", "tensor")),
            P("section", "dp", "tensor"),
            P("section", "dp", "tensor"),
            P("section", "dp", "tensor"),
            P("section", "tensor", "dp"),
            P("section", ("dp", "tensor")),
            P("section", "dp", "tensor"),
            P("section", "dp", "tensor"),
            P("section", "tensor", "dp"),
        ),
        check_vma=False,
    )
```

```python
import jax
import jax.numpy as jnp
from jax import lax
from jax.experimental import pallas as pl
from jax.experimental.pallas import tpu as pltpu
from jax.sharding import PartitionSpec as P

HEAD = 64


EPSILON = 1e-05
MASK_FILL = -1e30
BF16 = jnp.bfloat16
F32 = jnp.float32
LANES = 128
SCALE = HEAD ** (-0.5)
VMEM_BYTES = 12 * 2**20
GRADS_VMEM_BYTES = 20 * 2**20


def turn(value, axis, steps):
    count = lax.axis_size(axis)
    return lax.ppermute(value, axis, [(i, (i + steps) % count) for i in range(count)])


def swap(value):
    return lax.ppermute(value, "section", [(0, 1), (1, 0)])


def contract(left, right, left_dim, right_dim):
    return lax.dot_general(
        left, right, (((left_dim,), (right_dim,)), ((), ())), preferred_element_type=F32
    )


def geometry(seq_lens, rows):
    count = lax.axis_size("tensor")
    place = (lax.axis_index("tensor") - jnp.arange(count, dtype=jnp.int32)) % count
    row_ids = (place[:, None] * rows + jnp.arange(rows, dtype=jnp.int32)[None, :]).reshape(-1)
    ends = jnp.cumsum(seq_lens)
    starts = ends - seq_lens
    member = jnp.sum((row_ids[:, None] >= ends[None, :]).astype(jnp.int32), axis=1)
    slots = jnp.arange(seq_lens.shape[0], dtype=jnp.int32)
    begins = jnp.sum(jnp.where(member[:, None] == slots[None, :], starts[None, :], 0), axis=1)
    position = row_ids - begins
    half_dim = HEAD // 2
    frequency = 10000.0 ** (-jnp.arange(half_dim, dtype=F32) / half_dim)
    angle = position.astype(F32)[:, None] * frequency[None, :]
    allowed = (member[:, None] == member[None, :]) & (row_ids[:, None] >= row_ids[None, :])
    cosine, sine_part = (jnp.cos(angle), jnp.sin(angle))
    cosine = jnp.concatenate([cosine] * (LANES // half_dim), axis=1)
    sine_part = jnp.concatenate([-sine_part, sine_part] * (LANES // HEAD), axis=1)
    turned = jnp.arange(LANES) < HEAD
    tables = jnp.stack(
        [cosine, sine_part, jnp.where(turned, cosine, 1.0), jnp.where(turned, sine_part, 0.0)]
    )
    return (tables, jnp.where(allowed, 0.0, MASK_FILL))


def barrier(*values):
    return lax.optimization_barrier(values)


class Job:
    def __init__(self, fn, *inputs, held=()):
        self.fn, self.inputs, self.held, self.results = (fn, inputs, held, None)

    def __getitem__(self, which):
        return self.results[which]


def step(value, job):
    if job is None:
        return turn(value, "tensor", 1)
    inputs = job.inputs() if callable(job.inputs) else job.inputs
    value, *inputs = barrier(value, *inputs)
    results = job.fn(*inputs)
    recv, *values = barrier(turn(value, "tensor", 1), *results, *job.held)
    job.results, job.held = (values[: len(results)], values[len(results) :])
    return recv


def spread(block, jobs=(), parts=1):
    pieces = list(jnp.split(block, parts))
    for k in range(lax.axis_size("tensor") - 1):
        for _ in range(parts):
            pieces.append(step(pieces[-parts], jobs[k] if k < len(jobs) else None))
    return jnp.concatenate(pieces, axis=0)


def collect(partial, jobs=()):
    count = lax.axis_size("tensor")
    rows = partial.shape[0] // count
    blocks = partial.reshape(count, rows, partial.shape[1])
    total = blocks[1 % count]
    for k in range(count - 1):
        recv = step(total.astype(BF16), jobs[k] if k < len(jobs) else None)
        total = recv.astype(F32) + blocks[(k + 2) % count].astype(F32)
    return total


class Ring:
    def __init__(self, first):
        self.count, self.taken, self.value = (lax.axis_size("tensor"), 0, first)

    def run(self, fn, *inputs):
        if self.taken == self.count - 1:
            return fn(*inputs)
        job = Job(fn, *inputs)
        self.accept(step(self.value, job))
        self.taken += 1
        return tuple(job.results)

    def finish(self):
        while self.taken < self.count - 1:
            self.run(lambda: ())
        return self.result()


class SpreadRing(Ring):
    def __init__(self, block):
        super().__init__(block)
        self.pieces = [block]

    def accept(self, recv):
        self.pieces.append(recv)
        self.value = recv

    def result(self):
        return jnp.concatenate(self.pieces, axis=0)


class CollectRing(Ring):
    def __init__(self, partial):
        count = lax.axis_size("tensor")
        self.blocks = partial.reshape(count, partial.shape[0] // count, partial.shape[1])
        self.total = self.blocks[1 % count].astype(F32)
        super().__init__(self.total.astype(BF16))

    def accept(self, recv):
        block = self.blocks[(self.taken + 2) % self.count]
        self.total = recv.astype(F32) + block.astype(F32)
        self.value = self.total.astype(BF16)

    def result(self):
        return self.total


def estimate(us):
    return pl.CostEstimate(flops=0, bytes_accessed=int(us * 3.3e6), transcendentals=0)


def normalizer(rows):
    return lax.rsqrt(jnp.mean(rows * rows, axis=1, keepdims=True) + EPSILON)


def half_swap(x):
    lane = lax.broadcasted_iota(jnp.int32, x.shape, 1)
    first = (lane % HEAD) < HEAD // 2
    return jnp.where(
        first, pltpu.roll(x, LANES - HEAD // 2, 1), pltpu.roll(x, HEAD // 2, 1)
    )


def heads_of(kv):
    low = lax.broadcasted_iota(jnp.int32, kv.shape, 1) < HEAD
    kv = kv.astype(F32)
    turned = pltpu.roll(kv, HEAD, 1)
    keys = (jnp.where(low, kv, 0.0).astype(BF16), jnp.where(low, 0.0, turned).astype(BF16))
    values = (jnp.where(low, turned, 0.0).astype(BF16), jnp.where(low, 0.0, kv).astype(BF16))
    return (keys, values)


def attend_kernel(qkv_ref, table_ref, bias_ref, rot_ref, mixed_ref, lse_ref):
    q_cols = mixed_ref.shape[1]
    cosine, sine_part = (table_ref[0], table_ref[1])
    kv = qkv_ref[:, q_cols:]
    kv = (kv * table_ref[2] + half_swap(kv) * table_ref[3]).astype(BF16)
    rot_ref[:, q_cols:] = kv
    keys, values = heads_of(kv)
    bias = bias_ref[...]
    head_ids = lax.broadcasted_iota(jnp.int32, lse_ref.shape, 1)

    def one_slab(slab, log_totals):
        cols = pl.ds(pl.multiple_of(slab * LANES, LANES), LANES)
        query = qkv_ref[:, cols]
        query = (query * cosine + half_swap(query) * sine_part).astype(BF16)
        rot_ref[:, cols] = query
        mixed = 0.0
        for odd in range(2):
            scores = contract(query, keys[odd], 1, 1) * SCALE + bias
            row_max = jnp.max(scores, axis=1, keepdims=True)
            exponent = jnp.exp(scores - row_max)
            totals = jnp.sum(exponent, axis=1, keepdims=True)
            log_total = row_max + jnp.log(totals)
            log_totals = jnp.where(head_ids == 2 * slab + odd, log_total, log_totals)
            mixed = mixed + contract((exponent / totals).astype(BF16), values[odd], 1, 0)
        mixed_ref[:, cols] = mixed.astype(BF16)
        return log_totals

    lse_ref[...] = lax.fori_loop(
        0, q_cols // LANES, one_slab, jnp.zeros(lse_ref.shape, F32)
    )


def attend(normed_one, geo, w_attn, q_cols, kv_cols):
    group = normed_one.shape[0]
    both = q_cols + 2 * kv_cols
    qkv = jnp.dot(normed_one, w_attn[:, :both], preferred_element_type=F32)
    rotated, mixed, log_total = pl.pallas_call(
        attend_kernel,
        out_shape=(
            jax.ShapeDtypeStruct((group, both), BF16),
            jax.ShapeDtypeStruct((group, q_cols), BF16),
            jax.ShapeDtypeStruct((group, q_cols // HEAD), F32),
        ),
        cost_estimate=estimate(3),
        compiler_params=pltpu.CompilerParams(vmem_limit_bytes=VMEM_BYTES),
    )(qkv, *geo)
    out_term = contract(mixed, w_attn[:, both : both + q_cols], 1, 1).astype(BF16)
    return (out_term, rotated, log_total, mixed)


def attend_back_kernel(d_mixed_ref, rot_ref, lse_ref, table_ref, bias_ref, out_ref):
    q_cols = d_mixed_ref.shape[1]
    cosine, sine_part = (table_ref[0], table_ref[1])
    keys, values = heads_of(rot_ref[:, q_cols:])
    bias = bias_ref[...]
    log_totals = lse_ref[...]
    head_ids = lax.broadcasted_iota(jnp.int32, log_totals.shape, 1)

    def one_slab(slab, sums):
        d_keys, d_values = (list(sums[:2]), list(sums[2:]))
        cols = pl.ds(pl.multiple_of(slab * LANES, LANES), LANES)
        query = rot_ref[:, cols]
        d_mixed = d_mixed_ref[:, cols]
        d_query = 0.0
        for odd in range(2):
            log_total = jnp.sum(
                jnp.where(head_ids == 2 * slab + odd, log_totals, 0.0), axis=1, keepdims=True
            )
            scores = contract(query, keys[odd], 1, 1) * SCALE + bias
            probs = jnp.exp(scores - log_total)
            d_probs = contract(d_mixed, values[odd], 1, 1)
            total = jnp.sum(d_probs * probs, axis=1, keepdims=True)
            d_scores = (probs * (d_probs - total)).astype(BF16)
            d_query = d_query + contract(d_scores, keys[odd], 1, 0)
            d_values[odd] = d_values[odd] + contract(probs.astype(BF16), d_mixed, 0, 0)
            d_keys[odd] = d_keys[odd] + contract(d_scores, query, 0, 0)
        d_query = d_query * SCALE
        out_ref[:, cols] = (d_query * cosine - half_swap(d_query) * sine_part).astype(BF16)
        return (*d_keys, *d_values)

    zeros = jnp.zeros((d_mixed_ref.shape[0], LANES), F32)
    sums = lax.fori_loop(0, q_cols // LANES, one_slab, (zeros,) * 4)
    d_keys, d_values = (sums[:2], sums[2:])
    low = lax.broadcasted_iota(jnp.int32, d_keys[0].shape, 1) < HEAD
    d_kv = jnp.where(
        low,
        (d_keys[0] + pltpu.roll(d_keys[1], HEAD, 1)) * SCALE,
        d_values[1] + pltpu.roll(d_values[0], HEAD, 1),
    )
    d_kv = d_kv * table_ref[2] - half_swap(d_kv) * table_ref[3]
    out_ref[:, q_cols:] = d_kv.astype(BF16)


def attend_back(grad_attn, geo, w_attn, at_first, rotated, log_total):
    other_attn = swap(core_half(grad_attn, at_first, False))
    both = rotated.shape[1]
    q_cols = log_total.shape[1] * HEAD
    w_out = w_attn[:, both : both + q_cols]
    d_mixed = jnp.dot(grad_attn, w_out, preferred_element_type=F32).astype(BF16)
    d_qkv = pl.pallas_call(
        attend_back_kernel,
        out_shape=jax.ShapeDtypeStruct(rotated.shape, BF16),
        cost_estimate=estimate(6),
        compiler_params=pltpu.CompilerParams(vmem_limit_bytes=VMEM_BYTES),
    )(d_mixed, rotated, log_total, *geo)
    d_norm_one = contract(d_qkv, w_attn[:, :both], 1, 1).astype(BF16)
    return (d_qkv, swap(d_qkv), other_attn, d_norm_one)


def feed(normed_two, w_ffn, units):
    gate_up = jnp.dot(normed_two, w_ffn[:, : 2 * units], preferred_element_type=F32)
    hidden = (jax.nn.silu(gate_up[:, :units]) * gate_up[:, units:]).astype(BF16)
    return (gate_up, hidden)


def feed_back(grad_feed, gate_up, w_ffn):
    units = gate_up.shape[1] // 2
    d_hidden = jnp.dot(grad_feed, w_ffn[:, 2 * units :], preferred_element_type=F32)
    gate, up = (gate_up[:, :units], gate_up[:, units:])
    sigmoid_gate = jax.nn.sigmoid(gate)
    d_up = (d_hidden * gate * sigmoid_gate).astype(BF16)
    d_gate = (d_hidden * up * sigmoid_gate * (1.0 + gate * (1.0 - sigmoid_gate))).astype(BF16)
    return (jnp.concatenate([d_gate, d_up], axis=1),)


def feed_back_rows(d_gate_up, w_ffn):
    return (contract(d_gate_up, w_ffn[:, : d_gate_up.shape[1]], 1, 1),)


def core_half(rows, at_first, own):
    width = rows.shape[1] // (2 * lax.axis_size("dp"))
    low, high = (
        jnp.concatenate(
            [rows[:, start : start + width] for start in range(first, rows.shape[1], 2 * width)],
            axis=1,
        )
        for first in (0, width)
    )
    return jnp.where(at_first, low, high) if own else jnp.where(at_first, high, low)


def exchange(at_first, rows, *whole):
    return tuple(swap(core_half(x, at_first, False)) for x in rows) + tuple(map(swap, whole))


def weight_grads_kernel(_, *refs):
    *pairs, out_ref = refs
    at = 0
    for k in range(0, len(pairs), 4):
        rows, other_rows, grads, other_grads = (ref[...] for ref in pairs[k : k + 4])
        total = contract(rows, grads, 0, 0) + contract(other_rows, other_grads, 0, 0)
        out_ref[:, at : at + total.shape[1]] = total.astype(BF16)
        at += total.shape[1]


def weight_grads(at_first, *pairs):
    group, half = pairs[0][1].shape
    n_dp = lax.axis_size("dp")
    tile = half // n_dp
    direct = tile % LANES == 0
    if not direct:
        pairs = [(core_half(rows, at_first, True), *rest) for rows, *rest in pairs]
        tile = min(256, half)
    specs = []
    for _, _, grads, _ in pairs:
        own_spec = pl.BlockSpec((group, tile), lambda i, core: (0, 2 * i + core[0]))
        half_spec = pl.BlockSpec((group, tile), lambda i, core: (0, i))
        grads_spec = pl.BlockSpec(
            (group, grads.shape[1]), lambda i, core: (0, 0), pipeline_mode=pl.Buffered(1)
        )
        specs += [own_spec if direct else half_spec, half_spec, grads_spec, grads_spec]
    total = sum(grads.shape[1] for _, _, grads, _ in pairs)
    return pl.pallas_call(
        weight_grads_kernel,
        grid_spec=pltpu.PrefetchScalarGridSpec(
            num_scalar_prefetch=1,
            grid=(half // tile,),
            in_specs=specs,
            out_specs=pl.BlockSpec((tile, total), lambda i, core: (i, 0)),
        ),
        out_shape=pltpu.HBM((half, total), BF16),
        cost_estimate=estimate(total / 330),
        compiler_params=pltpu.CompilerParams(vmem_limit_bytes=GRADS_VMEM_BYTES),
    )(
        jnp.where(at_first, 0, 1).astype(jnp.int32).reshape(1),
        *[x for pair in pairs for x in pair],
    )


def scatter(half):
    return lax.psum_scatter(half, "dp", scatter_dimension=0, tiled=True)


def norm_back(rows, inverse, gain, d_normed):
    unit = rows * inverse
    scaled = d_normed * gain
    return inverse * (scaled - unit * jnp.mean(scaled * unit, axis=1, keepdims=True))


def backward(
    kept, grad_all, grad, geo, weights, at_first, others, early, aside, down_job
):
    (layer_in, normed_one, rotated, log_total, mixed, middle, normed_two, gate_up, hidden) = kept
    norm_gain, ffn_gain, w_attn, w_ffn = weights
    last = down_job is None
    run = aside.run if aside else lambda fn, *inputs: fn(*inputs)
    (d_gate_up,) = run(feed_back, grad_all, gate_up, w_ffn)
    (d_norm_two_all,) = run(feed_back_rows, d_gate_up, w_ffn)
    if last:
        d_gate_up, grad_all = barrier(d_gate_up, grad_all)
        others["grad_all"] = exchange(at_first, (grad_all,))[0]

    def grads(*given):
        pairs = [given[k : k + 4] for k in range(0, len(given), 4)]
        return (weight_grads(at_first, *pairs),)

    if last:
        pairs = (
            *(normed_two, others["normed_two"], d_gate_up, swap(d_gate_up)),
            *(grad_all, others["grad_all"], hidden, others["hidden"]),
        )
        d_norm_two_all, *pairs = barrier(d_norm_two_all, *pairs)
        grads_jobs = (Job(grads, *pairs), Job(lambda: (), held=early))
        d_norm_two = collect(d_norm_two_all, grads_jobs)
        early = grads_jobs[1].held
    else:
        swap_job = Job(
            lambda d_gate_up, hidden, *rows: (
                swap(d_gate_up), swap(hidden), *exchange(at_first, rows)
            ),
            d_gate_up,
            hidden,
            normed_two,
            grad_all,
        )
        grads_jobs = (Job(grads), Job(grads))
        grads_jobs[0].inputs = lambda: (normed_two, swap_job[2], d_gate_up, swap_job[0])
        grads_jobs[1].inputs = lambda: (grad_all, swap_job[3], hidden, swap_job[1])
        d_norm_two = collect(d_norm_two_all, (swap_job, *grads_jobs))
    reduced = [scatter(job[0]) for job in grads_jobs if job.results]
    d_middle = grad.astype(F32) + norm_back(middle, normalizer(middle), ffn_gain, d_norm_two)
    ffn_gain_job = Job(
        lambda d_all, normed: (
            jnp.sum(d_all.astype(F32) * (normed.astype(F32) / ffn_gain), axis=0),
        ),
        d_norm_two_all,
        normed_two,
    )
    if last:
        aside_job = Job(lambda value: (turn(value, "tensor", 1),), aside.value)
        grad_attn = spread(d_middle.astype(BF16), (ffn_gain_job, aside_job))
        aside.accept(aside_job[0])
        aside.taken += 1
    else:
        grad_attn = spread(d_middle.astype(BF16), (ffn_gain_job, down_job))
        aside = CollectRing(down_job[0])
    d_qkv, other_qkv, other_attn, d_norm_one_all = attend_back(
        grad_attn, geo, w_attn, at_first, rotated, log_total
    )
    other_one, other_mixed = others.get("attn") or exchange(at_first, (normed_one,), mixed)
    pairs = (
        *(normed_one, other_one, d_qkv, other_qkv),
        *(grad_attn, other_attn, mixed, other_mixed),
    )
    d_norm_one_all, *pairs = barrier(d_norm_one_all, *pairs)
    attn_job = Job(grads, *pairs, held=reduced[:1] if last else ())
    attn_gain_job = Job(
        lambda d_all, normed: (
            jnp.sum(d_all.astype(F32) * (normed.astype(F32) / norm_gain), axis=0),
        ),
        d_norm_one_all,
        normed_one,
    )
    last_job = Job(lambda: (), held=() if last else reduced[:1])
    d_norm_one = collect(d_norm_one_all, (attn_job, attn_gain_job, last_job))
    reduced[:1] = attn_job.held or last_job.held
    g_attn = attn_job[0]
    d_input = d_middle + norm_back(layer_in, normalizer(layer_in), norm_gain, d_norm_one)
    gain_grads = jnp.stack([attn_gain_job[0], ffn_gain_job[0]])
    return (d_input.astype(BF16), (scatter(g_attn), *reduced), gain_grads, early, aside)


def both_layers(own, at_first):
    rows = own.shape[0] // 2
    low, high = (own[:rows], own[rows:])
    mine = jnp.where(at_first, low, high)
    got = swap(jnp.where(at_first, high, low))
    return (jnp.where(at_first, mine, got), jnp.where(at_first, got, mine))


def own_layer(first, second, at_first):
    mine = jnp.where(at_first, first, second)
    got = swap(jnp.where(at_first, second, first))
    return jnp.concatenate([jnp.where(at_first, mine, got), jnp.where(at_first, got, mine)], axis=0)


def gather(shard):
    return lax.all_gather(shard, ("dp", "section"), axis=0, tiled=True)


def reduce_small(rows):
    for axis in ("tensor", "dp"):
        count = lax.axis_size(axis)
        if axis == "tensor":
            parts = rows.reshape(rows.shape[0], lax.axis_size("dp"), count, -1).transpose(2, 0, 1, 3)
        else:
            parts = rows.transpose(1, 0, 2)
        me = lax.axis_index(axis)
        rows = lax.dynamic_index_in_dim(parts, me, 0, keepdims=False)
        for k in range(1, count):
            part = lax.dynamic_index_in_dim(parts, (me + k) % count, 0, keepdims=False)
            rows = rows + turn(part, axis, k)
    return rows + swap(rows)


def local(
    tokens_in,
    cotangent,
    lengths,
    attn_gain,
    w_query,
    w_key,
    w_value,
    w_out,
    ffn_gain,
    w_gate,
    w_up,
    w_down,
):
    at_first = lax.axis_index("section") == 0
    rows = tokens_in.shape[1]
    q_cols, kv_cols, units = (w_query.shape[2], w_key.shape[2], w_gate.shape[2])
    tokens = jnp.where(at_first, tokens_in[0], tokens_in[1])
    upstream = jnp.where(at_first, cotangent[0], cotangent[1])
    gains_cols = jnp.pad(
        jnp.concatenate([attn_gain, ffn_gain], axis=0).T, ((0, 0), (0, LANES - 2))
    )
    attn_rows = jnp.concatenate(
        [w_query[0], w_key[0], w_value[0], w_out[0].T, gains_cols], axis=1
    )
    attn_rows, tokens = barrier(attn_rows, tokens)
    attn_parts = both_layers(attn_rows, at_first)
    prepare = Job(
        lambda gate, up, down: both_layers(
            jnp.concatenate([gate, up, down.T], axis=1), at_first
        ),
        w_gate[0],
        w_up[0],
        w_down[0],
    )
    tokens_all = spread(tokens, (None, prepare))
    tokens_all, upstream = barrier(tokens_all, upstream)
    upstream_ring = SpreadRing(upstream)
    first_attn = gather(attn_parts[0])
    first_ffn = gather(prepare[0])
    w_attns = [first_attn, gather(attn_parts[1])]
    w_ffns = [first_ffn]
    geo = geometry(jnp.where(at_first, lengths[0, 0], lengths[1, 0]), rows)
    tokens_all = tokens_all.astype(F32)
    layer_in = tokens.astype(F32)
    layers = []
    for layer in range(2):
        w_attn, w_ffn = (w_attns[layer], w_ffns[layer])
        norm_gain, ffn_gain = (
            w_attn[:, 2 * (q_cols + kv_cols) :][:, :2].T.astype(F32)
        )
        if layer:
            normed_one = spread(
                (layer_in * normalizer(layer_in) * norm_gain).astype(BF16), parts=2
            )
        else:
            normed_one = (tokens_all * normalizer(tokens_all) * norm_gain).astype(BF16)
        attention = (lambda normed, w: attend(normed, geo, w, q_cols, kv_cols), normed_one, w_attn)
        out_term, rotated, log_total, mixed = upstream_ring.run(*attention)
        middle = layer_in + collect(out_term)
        normed_two = spread((middle * normalizer(middle) * ffn_gain).astype(BF16), parts=2)
        others = {}
        if layer == 0:
            normed_two, upstream_ring.value = barrier(normed_two, upstream_ring.value)
            others.update(
                attn=upstream_ring.run(
                    lambda one, heads: exchange(at_first, (one,), heads), normed_one, mixed
                )
            )
            normed_two, upstream_ring.value = barrier(normed_two, upstream_ring.value)
        gate_up, hidden = feed(normed_two, w_ffn, units)
        down_job = Job(
            lambda hidden, w: (contract(hidden, w[:, 2 * units :], 1, 1).astype(BF16),),
            hidden,
            w_ffn,
        )
        if layer == 0:
            (down_term,) = down_job.fn(*down_job.inputs)
            ffn_swap = Job(
                lambda two, units: exchange(at_first, (two,), units), normed_two, hidden
            )
            first_out = (middle + collect(down_term, (None, ffn_swap))).astype(BF16)
            others.update(normed_two=ffn_swap[0], hidden=ffn_swap[1])
            first_out, ffn_part = barrier(first_out, prepare[1])
            w_ffns.append(gather(ffn_part))
        kept = (
            layer_in, normed_one, rotated, log_total, mixed, middle, normed_two, gate_up, hidden
        )
        layers.append((kept, (norm_gain, ffn_gain, w_attn, w_ffn), others))
        layer_in = first_out.astype(F32)

    def back(layer, grad_all, grad, early, aside, down_job):
        kept, weights, others = layers[layer]
        return backward(
            kept,
            grad_all,
            grad,
            geo,
            weights,
            at_first,
            others,
            early,
            aside,
            down_job,
        )

    upstream_all = upstream_ring.finish()
    d_second, (second_attn, second_ffn, second_down), second_gains, _, out_ring = back(
        1, upstream_all, upstream, (), None, down_job
    )
    down_done = Job(lambda: (), held=(second_down,))
    d_second_all = spread(d_second, (None, down_done))
    d_first, (first_attn, first_ffn), first_gains, (second_attn,), _ = back(
        0, d_second_all, d_second, (second_attn,), out_ring, None
    )
    second_out = (middle + out_ring.finish()).astype(BF16)
    second_ffn = jnp.concatenate([second_ffn, *down_done.held], axis=1)
    g_gains = reduce_small(jnp.concatenate([first_gains, second_gains]))
    gain_own = jnp.where(at_first, g_gains[:2], g_gains[2:])

    def by_layer(first, second):
        mine = jnp.where(at_first, first, second)
        got = swap(jnp.where(at_first, second, first))
        return jnp.stack([jnp.where(at_first, mine, got), jnp.where(at_first, got, mine)])

    section_out = by_layer(first_out, second_out)
    input_grad = by_layer(d_first, d_second)
    g_ffn = own_layer(first_ffn, second_ffn, at_first).astype(F32)
    g_gate, g_up, g_down = (
        g_ffn[:, :units], g_ffn[:, units : 2 * units], g_ffn[:, 2 * units :].T
    )
    first_attn, gain_own, section_out, input_grad, g_gate, g_up, g_down = barrier(
        first_attn, gain_own, section_out, input_grad, g_gate, g_up, g_down
    )
    g_attn = own_layer(first_attn, second_attn, at_first).astype(F32)
    qkv = q_cols + 2 * kv_cols
    g_key_value = g_attn[:, q_cols:qkv].T
    return (
        section_out[None],
        input_grad[None],
        gain_own[0][None],
        g_attn[:, :q_cols][None],
        g_key_value[:kv_cols].T[None],
        g_key_value[kv_cols:].T[None],
        g_attn[:, qkv:].T[None],
        gain_own[1][None],
        g_gate[None],
        g_up[None],
        g_down[None],
    )


def solution(mesh):
    return jax.shard_map(
        local,
        mesh=mesh,
        in_specs=(
            P(None, ("dp", "tensor"), None),
            P(None, ("dp", "tensor"), None),
            P(None, "dp", None),
            P("section", "dp"),
            P("section", "dp", "tensor"),
            P("section", "dp", "tensor"),
            P("section", "dp", "tensor"),
            P("section", "tensor", "dp"),
            P("section", "dp"),
            P("section", "dp", "tensor"),
            P("section", "dp", "tensor"),
            P("section", "tensor", "dp"),
        ),
        out_specs=(
            P("section", None, ("dp", "tensor"), None),
            P("section", None, ("dp", "tensor"), None),
            P("section", ("dp", "tensor")),
            P("section", "dp", "tensor"),
            P("section", "dp", "tensor"),
            P("section", "dp", "tensor"),
            P("section", "tensor", "dp"),
            P("section", ("dp", "tensor")),
            P("section", "dp", "tensor"),
            P("section", "dp", "tensor"),
            P("section", "tensor", "dp"),
        ),
        check_vma=False,
    )
```

```python
import jax
import jax.numpy as jnp
from jax import lax
from jax.experimental import pallas as pl
from jax.experimental.pallas import tpu as pltpu
from jax.sharding import PartitionSpec as P

HEAD = 64


EPSILON = 1e-05
MASK_FILL = -1e30
BF16 = jnp.bfloat16
F32 = jnp.float32
LANES = 128
SCALE = HEAD ** (-0.5)
VMEM_BYTES = 12 * 2**20
GRADS_VMEM_BYTES = 20 * 2**20


def turn(value, axis, steps):
    count = lax.axis_size(axis)
    return lax.ppermute(value, axis, [(i, (i + steps) % count) for i in range(count)])


def swap(value):
    return lax.ppermute(value, "section", [(0, 1), (1, 0)])


def contract(left, right, left_dim, right_dim):
    return lax.dot_general(
        left, right, (((left_dim,), (right_dim,)), ((), ())), preferred_element_type=F32
    )


def geometry(seq_lens, rows):
    count = lax.axis_size("tensor")
    place = (lax.axis_index("tensor") - jnp.arange(count, dtype=jnp.int32)) % count
    row_ids = (place[:, None] * rows + jnp.arange(rows, dtype=jnp.int32)[None, :]).reshape(-1)
    ends = jnp.cumsum(seq_lens)
    starts = ends - seq_lens
    member = jnp.sum((row_ids[:, None] >= ends[None, :]).astype(jnp.int32), axis=1)
    slots = jnp.arange(seq_lens.shape[0], dtype=jnp.int32)
    begins = jnp.sum(jnp.where(member[:, None] == slots[None, :], starts[None, :], 0), axis=1)
    position = row_ids - begins
    half_dim = HEAD // 2
    frequency = 10000.0 ** (-jnp.arange(half_dim, dtype=F32) / half_dim)
    angle = position.astype(F32)[:, None] * frequency[None, :]
    allowed = (member[:, None] == member[None, :]) & (row_ids[:, None] >= row_ids[None, :])
    cosine, sine_part = (jnp.cos(angle), jnp.sin(angle))
    cosine = jnp.concatenate([cosine] * (LANES // half_dim), axis=1)
    sine_part = jnp.concatenate([-sine_part, sine_part] * (LANES // HEAD), axis=1)
    turned = jnp.arange(LANES) < HEAD
    tables = jnp.stack(
        [cosine, sine_part, jnp.where(turned, cosine, 1.0), jnp.where(turned, sine_part, 0.0)]
    )
    return (tables, jnp.where(allowed, 0.0, MASK_FILL))


def barrier(*values):
    return lax.optimization_barrier(values)


class Job:
    def __init__(self, fn, *inputs, held=()):
        self.fn, self.inputs, self.held, self.results = (fn, inputs, held, None)

    def __getitem__(self, which):
        return self.results[which]


def step(value, job):
    if job is None:
        return turn(value, "tensor", 1)
    inputs = job.inputs() if callable(job.inputs) else job.inputs
    value, *inputs = barrier(value, *inputs)
    results = job.fn(*inputs)
    recv, *values = barrier(turn(value, "tensor", 1), *results, *job.held)
    job.results, job.held = (values[: len(results)], values[len(results) :])
    return recv


def spread(block, jobs=(), parts=1):
    pieces = list(jnp.split(block, parts))
    for k in range(lax.axis_size("tensor") - 1):
        for _ in range(parts):
            pieces.append(step(pieces[-parts], jobs[k] if k < len(jobs) else None))
    return jnp.concatenate(pieces, axis=0)


def collect(partial, jobs=()):
    count = lax.axis_size("tensor")
    rows = partial.shape[0] // count
    blocks = partial.reshape(count, rows, partial.shape[1])
    total = blocks[1 % count]
    for k in range(count - 1):
        recv = step(total.astype(BF16), jobs[k] if k < len(jobs) else None)
        total = recv.astype(F32) + blocks[(k + 2) % count].astype(F32)
    return total


class Ring:
    def __init__(self, first):
        self.count, self.taken, self.value = (lax.axis_size("tensor"), 0, first)

    def run(self, fn, *inputs):
        if self.taken == self.count - 1:
            return fn(*inputs)
        job = Job(fn, *inputs)
        self.accept(step(self.value, job))
        self.taken += 1
        return tuple(job.results)

    def finish(self):
        while self.taken < self.count - 1:
            self.run(lambda: ())
        return self.result()


class SpreadRing(Ring):
    def __init__(self, block):
        super().__init__(block)
        self.pieces = [block]

    def accept(self, recv):
        self.pieces.append(recv)
        self.value = recv

    def result(self):
        return jnp.concatenate(self.pieces, axis=0)


class CollectRing(Ring):
    def __init__(self, partial):
        count = lax.axis_size("tensor")
        self.blocks = partial.reshape(count, partial.shape[0] // count, partial.shape[1])
        self.total = self.blocks[1 % count].astype(F32)
        super().__init__(self.total.astype(BF16))

    def accept(self, recv):
        block = self.blocks[(self.taken + 2) % self.count]
        self.total = recv.astype(F32) + block.astype(F32)
        self.value = self.total.astype(BF16)

    def result(self):
        return self.total


def estimate(us):
    return pl.CostEstimate(flops=0, bytes_accessed=int(us * 3.3e6), transcendentals=0)


def normalizer(rows):
    return lax.rsqrt(jnp.mean(rows * rows, axis=1, keepdims=True) + EPSILON)


def half_swap(x):
    lane = lax.broadcasted_iota(jnp.int32, x.shape, 1)
    first = (lane % HEAD) < HEAD // 2
    return jnp.where(
        first, pltpu.roll(x, LANES - HEAD // 2, 1), pltpu.roll(x, HEAD // 2, 1)
    )


def heads_of(kv):
    low = lax.broadcasted_iota(jnp.int32, kv.shape, 1) < HEAD
    kv = kv.astype(F32)
    turned = pltpu.roll(kv, HEAD, 1)
    keys = (jnp.where(low, kv, 0.0).astype(BF16), jnp.where(low, 0.0, turned).astype(BF16))
    values = (jnp.where(low, turned, 0.0).astype(BF16), jnp.where(low, 0.0, kv).astype(BF16))
    return (keys, values)


def attend_kernel(qkv_ref, table_ref, bias_ref, rot_ref, mixed_ref, lse_ref):
    q_cols = mixed_ref.shape[1]
    cosine, sine_part = (table_ref[0], table_ref[1])
    kv = qkv_ref[:, q_cols:]
    kv = (kv * table_ref[2] + half_swap(kv) * table_ref[3]).astype(BF16)
    rot_ref[:, q_cols:] = kv
    keys, values = heads_of(kv)
    bias = bias_ref[...]
    head_ids = lax.broadcasted_iota(jnp.int32, lse_ref.shape, 1)

    def one_slab(slab, log_totals):
        cols = pl.ds(pl.multiple_of(slab * LANES, LANES), LANES)
        query = qkv_ref[:, cols]
        query = (query * cosine + half_swap(query) * sine_part).astype(BF16)
        rot_ref[:, cols] = query
        mixed = 0.0
        for odd in range(2):
            scores = contract(query, keys[odd], 1, 1) * SCALE + bias
            row_max = jnp.max(scores, axis=1, keepdims=True)
            exponent = jnp.exp(scores - row_max)
            totals = jnp.sum(exponent, axis=1, keepdims=True)
            log_total = row_max + jnp.log(totals)
            log_totals = jnp.where(head_ids == 2 * slab + odd, log_total, log_totals)
            mixed = mixed + contract((exponent / totals).astype(BF16), values[odd], 1, 0)
        mixed_ref[:, cols] = mixed.astype(BF16)
        return log_totals

    lse_ref[...] = lax.fori_loop(
        0, q_cols // LANES, one_slab, jnp.zeros(lse_ref.shape, F32)
    )


def attend(normed_one, geo, w_attn, q_cols, kv_cols):
    group = normed_one.shape[0]
    both = q_cols + 2 * kv_cols
    qkv = jnp.dot(normed_one, w_attn[:, :both], preferred_element_type=F32)
    rotated, mixed, log_total = pl.pallas_call(
        attend_kernel,
        out_shape=(
            jax.ShapeDtypeStruct((group, both), BF16),
            jax.ShapeDtypeStruct((group, q_cols), BF16),
            jax.ShapeDtypeStruct((group, q_cols // HEAD), F32),
        ),
        cost_estimate=estimate(3),
        compiler_params=pltpu.CompilerParams(vmem_limit_bytes=VMEM_BYTES),
    )(qkv, *geo)
    out_term = contract(mixed, w_attn[:, both : both + q_cols], 1, 1).astype(BF16)
    return (out_term, rotated, log_total, mixed)


def attend_back_kernel(d_mixed_ref, rot_ref, lse_ref, table_ref, bias_ref, out_ref):
    q_cols = d_mixed_ref.shape[1]
    cosine, sine_part = (table_ref[0], table_ref[1])
    keys, values = heads_of(rot_ref[:, q_cols:])
    bias = bias_ref[...]
    log_totals = lse_ref[...]
    head_ids = lax.broadcasted_iota(jnp.int32, log_totals.shape, 1)

    def one_slab(slab, sums):
        d_keys, d_values = (list(sums[:2]), list(sums[2:]))
        cols = pl.ds(pl.multiple_of(slab * LANES, LANES), LANES)
        query = rot_ref[:, cols]
        d_mixed = d_mixed_ref[:, cols]
        d_query = 0.0
        for odd in range(2):
            log_total = jnp.sum(
                jnp.where(head_ids == 2 * slab + odd, log_totals, 0.0), axis=1, keepdims=True
            )
            scores = contract(query, keys[odd], 1, 1) * SCALE + bias
            probs = jnp.exp(scores - log_total)
            d_probs = contract(d_mixed, values[odd], 1, 1)
            total = jnp.sum(d_probs * probs, axis=1, keepdims=True)
            d_scores = (probs * (d_probs - total)).astype(BF16)
            d_query = d_query + contract(d_scores, keys[odd], 1, 0)
            d_values[odd] = d_values[odd] + contract(probs.astype(BF16), d_mixed, 0, 0)
            d_keys[odd] = d_keys[odd] + contract(d_scores, query, 0, 0)
        d_query = d_query * SCALE
        out_ref[:, cols] = (d_query * cosine - half_swap(d_query) * sine_part).astype(BF16)
        return (*d_keys, *d_values)

    zeros = jnp.zeros((d_mixed_ref.shape[0], LANES), F32)
    sums = lax.fori_loop(0, q_cols // LANES, one_slab, (zeros,) * 4)
    d_keys, d_values = (sums[:2], sums[2:])
    low = lax.broadcasted_iota(jnp.int32, d_keys[0].shape, 1) < HEAD
    d_kv = jnp.where(
        low,
        (d_keys[0] + pltpu.roll(d_keys[1], HEAD, 1)) * SCALE,
        d_values[1] + pltpu.roll(d_values[0], HEAD, 1),
    )
    d_kv = d_kv * table_ref[2] - half_swap(d_kv) * table_ref[3]
    out_ref[:, q_cols:] = d_kv.astype(BF16)


def attend_back(grad_attn, geo, w_attn, at_first, rotated, log_total):
    other_attn = swap(core_half(grad_attn, at_first, False))
    both = rotated.shape[1]
    q_cols = log_total.shape[1] * HEAD
    w_out = w_attn[:, both : both + q_cols]
    d_mixed = jnp.dot(grad_attn, w_out, preferred_element_type=F32).astype(BF16)
    d_qkv = pl.pallas_call(
        attend_back_kernel,
        out_shape=jax.ShapeDtypeStruct(rotated.shape, BF16),
        cost_estimate=estimate(6),
        compiler_params=pltpu.CompilerParams(vmem_limit_bytes=VMEM_BYTES),
    )(d_mixed, rotated, log_total, *geo)
    d_norm_one = contract(d_qkv, w_attn[:, :both], 1, 1).astype(BF16)
    return (d_qkv, swap(d_qkv), other_attn, d_norm_one)


def feed(normed_two, w_ffn, units):
    gate_up = jnp.dot(normed_two, w_ffn[:, : 2 * units], preferred_element_type=F32)
    hidden = (jax.nn.silu(gate_up[:, :units]) * gate_up[:, units:]).astype(BF16)
    return (gate_up, hidden)


def feed_back(grad_feed, gate_up, w_ffn):
    units = gate_up.shape[1] // 2
    d_hidden = jnp.dot(grad_feed, w_ffn[:, 2 * units :], preferred_element_type=F32)
    gate, up = (gate_up[:, :units], gate_up[:, units:])
    sigmoid_gate = jax.nn.sigmoid(gate)
    d_up = (d_hidden * gate * sigmoid_gate).astype(BF16)
    d_gate = (d_hidden * up * sigmoid_gate * (1.0 + gate * (1.0 - sigmoid_gate))).astype(BF16)
    return (jnp.concatenate([d_gate, d_up], axis=1),)


def feed_back_rows(d_gate_up, w_ffn):
    return (contract(d_gate_up, w_ffn[:, : d_gate_up.shape[1]], 1, 1),)


def core_half(rows, at_first, own):
    width = rows.shape[1] // (2 * lax.axis_size("dp"))
    low, high = (
        jnp.concatenate(
            [rows[:, start : start + width] for start in range(first, rows.shape[1], 2 * width)],
            axis=1,
        )
        for first in (0, width)
    )
    return jnp.where(at_first, low, high) if own else jnp.where(at_first, high, low)


def exchange(at_first, rows, *whole):
    return tuple(swap(core_half(x, at_first, False)) for x in rows) + tuple(map(swap, whole))


def weight_grads_kernel(_, *refs):
    *pairs, out_ref = refs
    at = 0
    for k in range(0, len(pairs), 4):
        rows, other_rows, grads, other_grads = (ref[...] for ref in pairs[k : k + 4])
        total = contract(rows, grads, 0, 0) + contract(other_rows, other_grads, 0, 0)
        out_ref[:, at : at + total.shape[1]] = total.astype(BF16)
        at += total.shape[1]


def weight_grads(at_first, *pairs):
    group, half = pairs[0][1].shape
    n_dp = lax.axis_size("dp")
    tile = half // n_dp
    direct = tile % LANES == 0
    if not direct:
        pairs = [(core_half(rows, at_first, True), *rest) for rows, *rest in pairs]
        tile = min(256, half)
    specs = []
    for _, _, grads, _ in pairs:
        own_spec = pl.BlockSpec((group, tile), lambda i, core: (0, 2 * i + core[0]))
        half_spec = pl.BlockSpec((group, tile), lambda i, core: (0, i))
        grads_spec = pl.BlockSpec(
            (group, grads.shape[1]), lambda i, core: (0, 0), pipeline_mode=pl.Buffered(1)
        )
        specs += [own_spec if direct else half_spec, half_spec, grads_spec, grads_spec]
    total = sum(grads.shape[1] for _, _, grads, _ in pairs)
    return pl.pallas_call(
        weight_grads_kernel,
        grid_spec=pltpu.PrefetchScalarGridSpec(
            num_scalar_prefetch=1,
            grid=(half // tile,),
            in_specs=specs,
            out_specs=pl.BlockSpec((tile, total), lambda i, core: (i, 0)),
        ),
        out_shape=pltpu.HBM((half, total), BF16),
        cost_estimate=estimate(total / 330),
        compiler_params=pltpu.CompilerParams(vmem_limit_bytes=GRADS_VMEM_BYTES),
    )(
        jnp.where(at_first, 0, 1).astype(jnp.int32).reshape(1),
        *[x for pair in pairs for x in pair],
    )


def scatter(half):
    return lax.psum_scatter(half, "dp", scatter_dimension=0, tiled=True)


def norm_back(rows, inverse, gain, d_normed):
    unit = rows * inverse
    scaled = d_normed * gain
    return inverse * (scaled - unit * jnp.mean(scaled * unit, axis=1, keepdims=True))


def backward(
    kept, grad_all, grad, geo, weights, at_first, others, early, aside, down_job
):
    (layer_in, normed_one, rotated, log_total, mixed, middle, normed_two, gate_up, hidden) = kept
    norm_gain, ffn_gain, w_attn, w_ffn = weights
    last = down_job is None
    run = aside.run if aside else lambda fn, *inputs: fn(*inputs)
    (d_gate_up,) = run(feed_back, grad_all, gate_up, w_ffn)
    (d_norm_two_all,) = run(feed_back_rows, d_gate_up, w_ffn)
    if last:
        d_gate_up, grad_all = barrier(d_gate_up, grad_all)
        others["grad_all"] = exchange(at_first, (grad_all,))[0]

    def grads(*given):
        pairs = [given[k : k + 4] for k in range(0, len(given), 4)]
        return (weight_grads(at_first, *pairs),)

    if last:
        pairs = (
            *(normed_two, others["normed_two"], d_gate_up, swap(d_gate_up)),
            *(grad_all, others["grad_all"], hidden, others["hidden"]),
        )
        d_norm_two_all, *pairs = barrier(d_norm_two_all, *pairs)
        grads_jobs = (Job(grads, *pairs), Job(lambda: (), held=early))
        d_norm_two = collect(d_norm_two_all, grads_jobs)
        early = grads_jobs[1].held
    else:
        swap_job = Job(
            lambda d_gate_up, hidden, *rows: (
                swap(d_gate_up), swap(hidden), *exchange(at_first, rows)
            ),
            d_gate_up,
            hidden,
            normed_two,
            grad_all,
        )
        grads_jobs = (Job(grads),)
        grads_jobs[0].inputs = lambda: (normed_two, swap_job[2], d_gate_up, swap_job[0])
        d_norm_two = collect(d_norm_two_all, (swap_job, *grads_jobs))
    reduced = [scatter(job[0]) for job in grads_jobs if job.results]
    d_middle = grad.astype(F32) + norm_back(middle, normalizer(middle), ffn_gain, d_norm_two)
    ffn_gain_job = Job(
        lambda d_all, normed: (
            jnp.sum(d_all.astype(F32) * (normed.astype(F32) / ffn_gain), axis=0),
        ),
        d_norm_two_all,
        normed_two,
    )
    if last:
        aside_job = Job(lambda value: (turn(value, "tensor", 1),), aside.value)
        grad_attn = spread(d_middle.astype(BF16), (ffn_gain_job, aside_job))
        aside.accept(aside_job[0])
        aside.taken += 1
    else:
        down_grad = Job(grads, grad_all, swap_job[3], hidden, swap_job[1])
        grad_attn = spread(d_middle.astype(BF16), (down_grad, down_job, ffn_gain_job))
        reduced.append(scatter(down_grad[0]))
        aside = CollectRing(down_job[0])
    d_qkv, other_qkv, other_attn, d_norm_one_all = attend_back(
        grad_attn, geo, w_attn, at_first, rotated, log_total
    )
    other_one, other_mixed = others.get("attn") or exchange(at_first, (normed_one,), mixed)
    pairs = (
        *(normed_one, other_one, d_qkv, other_qkv),
        *(grad_attn, other_attn, mixed, other_mixed),
    )
    d_norm_one_all, *pairs = barrier(d_norm_one_all, *pairs)
    attn_job = Job(grads, *pairs, held=reduced[:1] if last else ())
    attn_gain_job = Job(
        lambda d_all, normed: (
            jnp.sum(d_all.astype(F32) * (normed.astype(F32) / norm_gain), axis=0),
        ),
        d_norm_one_all,
        normed_one,
    )
    last_job = Job(lambda: (), held=() if last else reduced[:1])
    d_norm_one = collect(d_norm_one_all, (attn_job, attn_gain_job, last_job))
    reduced[:1] = attn_job.held or last_job.held
    g_attn = attn_job[0]
    d_input = d_middle + norm_back(layer_in, normalizer(layer_in), norm_gain, d_norm_one)
    gain_grads = jnp.stack([attn_gain_job[0], ffn_gain_job[0]])
    return (d_input.astype(BF16), (scatter(g_attn), *reduced), gain_grads, early, aside)


def both_layers(own, at_first):
    rows = own.shape[0] // 2
    low, high = (own[:rows], own[rows:])
    mine = jnp.where(at_first, low, high)
    got = swap(jnp.where(at_first, high, low))
    return (jnp.where(at_first, mine, got), jnp.where(at_first, got, mine))


def own_layer(first, second, at_first):
    mine = jnp.where(at_first, first, second)
    got = swap(jnp.where(at_first, second, first))
    return jnp.concatenate([jnp.where(at_first, mine, got), jnp.where(at_first, got, mine)], axis=0)


def gather(shard):
    return lax.all_gather(shard, ("dp", "section"), axis=0, tiled=True)


def reduce_small(rows):
    for axis in ("tensor", "dp"):
        count = lax.axis_size(axis)
        if axis == "tensor":
            parts = rows.reshape(rows.shape[0], lax.axis_size("dp"), count, -1).transpose(2, 0, 1, 3)
        else:
            parts = rows.transpose(1, 0, 2)
        me = lax.axis_index(axis)
        rows = lax.dynamic_index_in_dim(parts, me, 0, keepdims=False)
        for k in range(1, count):
            part = lax.dynamic_index_in_dim(parts, (me + k) % count, 0, keepdims=False)
            rows = rows + turn(part, axis, k)
    return rows + swap(rows)


def local(
    tokens_in,
    cotangent,
    lengths,
    attn_gain,
    w_query,
    w_key,
    w_value,
    w_out,
    ffn_gain,
    w_gate,
    w_up,
    w_down,
):
    at_first = lax.axis_index("section") == 0
    rows = tokens_in.shape[1]
    q_cols, kv_cols, units = (w_query.shape[2], w_key.shape[2], w_gate.shape[2])
    tokens = jnp.where(at_first, tokens_in[0], tokens_in[1])
    upstream = jnp.where(at_first, cotangent[0], cotangent[1])
    gains_cols = jnp.pad(
        jnp.concatenate([attn_gain, ffn_gain], axis=0).T, ((0, 0), (0, LANES - 2))
    )
    attn_rows = jnp.concatenate(
        [w_query[0], w_key[0], w_value[0], w_out[0].T, gains_cols], axis=1
    )
    attn_rows, tokens = barrier(attn_rows, tokens)
    attn_parts = both_layers(attn_rows, at_first)
    prepare = Job(
        lambda gate, up, down: both_layers(
            jnp.concatenate([gate, up, down.T], axis=1), at_first
        ),
        w_gate[0],
        w_up[0],
        w_down[0],
    )
    tokens_all = spread(tokens, (None, prepare))
    tokens_all, upstream = barrier(tokens_all, upstream)
    upstream_ring = SpreadRing(upstream)
    first_attn = gather(attn_parts[0])
    first_ffn = gather(prepare[0])
    w_attns = [first_attn, gather(attn_parts[1])]
    w_ffns = [first_ffn]
    geo = geometry(jnp.where(at_first, lengths[0, 0], lengths[1, 0]), rows)
    tokens_all = tokens_all.astype(F32)
    layer_in = tokens.astype(F32)
    layers = []
    for layer in range(2):
        w_attn, w_ffn = (w_attns[layer], w_ffns[layer])
        norm_gain, ffn_gain = (
            w_attn[:, 2 * (q_cols + kv_cols) :][:, :2].T.astype(F32)
        )
        if layer:
            normed_one = spread(
                (layer_in * normalizer(layer_in) * norm_gain).astype(BF16), parts=2
            )
        else:
            normed_one = (tokens_all * normalizer(tokens_all) * norm_gain).astype(BF16)
        attention = (lambda normed, w: attend(normed, geo, w, q_cols, kv_cols), normed_one, w_attn)
        out_term, rotated, log_total, mixed = upstream_ring.run(*attention)
        others = {}
        attn_jobs = ()
        if layer == 0:
            ring_job = Job(lambda value: (turn(value, "tensor", 1),), upstream_ring.value)
            attn_jobs = (None, ring_job)
        middle = layer_in + collect(out_term, attn_jobs)
        normed_two = spread((middle * normalizer(middle) * ffn_gain).astype(BF16), parts=2)
        if layer == 0:
            upstream_ring.accept(ring_job[0])
            upstream_ring.taken += 1
            swapped = exchange(at_first, barrier(normed_one, normed_two)[:1], mixed)
            normed_two, *swapped = barrier(normed_two, *swapped)
            others.update(attn=tuple(swapped))
        gate_up, hidden = feed(normed_two, w_ffn, units)
        down_job = Job(
            lambda hidden, w: (contract(hidden, w[:, 2 * units :], 1, 1).astype(BF16),),
            hidden,
            w_ffn,
        )
        if layer == 0:
            (down_term,) = down_job.fn(*down_job.inputs)
            ffn_swap = Job(
                lambda two, units: exchange(at_first, (two,), units), normed_two, hidden
            )
            first_out = (middle + collect(down_term, (None, ffn_swap))).astype(BF16)
            others.update(normed_two=ffn_swap[0], hidden=ffn_swap[1])
            first_out, ffn_part = barrier(first_out, prepare[1])
            w_ffns.append(gather(ffn_part))
        kept = (
            layer_in, normed_one, rotated, log_total, mixed, middle, normed_two, gate_up, hidden
        )
        layers.append((kept, (norm_gain, ffn_gain, w_attn, w_ffn), others))
        layer_in = first_out.astype(F32)

    def back(layer, grad_all, grad, early, aside, down_job):
        kept, weights, others = layers[layer]
        return backward(
            kept,
            grad_all,
            grad,
            geo,
            weights,
            at_first,
            others,
            early,
            aside,
            down_job,
        )

    upstream_all = upstream_ring.finish()
    d_second, (second_attn, second_ffn, second_down), second_gains, _, out_ring = back(
        1, upstream_all, upstream, (), None, down_job
    )
    down_done = Job(lambda: (), held=(second_down,))
    d_second_all = spread(d_second, (None, down_done))
    d_first, (first_attn, first_ffn), first_gains, (second_attn,), _ = back(
        0, d_second_all, d_second, (second_attn,), out_ring, None
    )
    second_out = (middle + out_ring.finish()).astype(BF16)
    second_ffn = jnp.concatenate([second_ffn, *down_done.held], axis=1)
    g_gains = reduce_small(jnp.concatenate([first_gains, second_gains]))
    gain_own = jnp.where(at_first, g_gains[:2], g_gains[2:])

    def by_layer(first, second):
        mine = jnp.where(at_first, first, second)
        got = swap(jnp.where(at_first, second, first))
        return jnp.stack([jnp.where(at_first, mine, got), jnp.where(at_first, got, mine)])

    section_out = by_layer(first_out, second_out)
    input_grad = by_layer(d_first, d_second)
    g_ffn = own_layer(first_ffn, second_ffn, at_first).astype(F32)
    g_gate, g_up, g_down = (
        g_ffn[:, :units], g_ffn[:, units : 2 * units], g_ffn[:, 2 * units :].T
    )
    first_attn, gain_own, section_out, input_grad, g_gate, g_up, g_down = barrier(
        first_attn, gain_own, section_out, input_grad, g_gate, g_up, g_down
    )
    g_attn = own_layer(first_attn, second_attn, at_first).astype(F32)
    qkv = q_cols + 2 * kv_cols
    g_key_value = g_attn[:, q_cols:qkv].T
    return (
        section_out[None],
        input_grad[None],
        gain_own[0][None],
        g_attn[:, :q_cols][None],
        g_key_value[:kv_cols].T[None],
        g_key_value[kv_cols:].T[None],
        g_attn[:, qkv:].T[None],
        gain_own[1][None],
        g_gate[None],
        g_up[None],
        g_down[None],
    )


def solution(mesh):
    return jax.shard_map(
        local,
        mesh=mesh,
        in_specs=(
            P(None, ("dp", "tensor"), None),
            P(None, ("dp", "tensor"), None),
            P(None, "dp", None),
            P("section", "dp"),
            P("section", "dp", "tensor"),
            P("section", "dp", "tensor"),
            P("section", "dp", "tensor"),
            P("section", "tensor", "dp"),
            P("section", "dp"),
            P("section", "dp", "tensor"),
            P("section", "dp", "tensor"),
            P("section", "tensor", "dp"),
        ),
        out_specs=(
            P("section", None, ("dp", "tensor"), None),
            P("section", None, ("dp", "tensor"), None),
            P("section", ("dp", "tensor")),
            P("section", "dp", "tensor"),
            P("section", "dp", "tensor"),
            P("section", "dp", "tensor"),
            P("section", "tensor", "dp"),
            P("section", ("dp", "tensor")),
            P("section", "dp", "tensor"),
            P("section", "dp", "tensor"),
            P("section", "tensor", "dp"),
        ),
        check_vma=False,
    )
```

```python
import jax
import jax.numpy as jnp
from jax import lax
from jax.experimental import pallas as pl
from jax.experimental.pallas import tpu as pltpu
from jax.sharding import PartitionSpec as P

HEAD = 64


EPSILON = 1e-05
MASK_FILL = -1e30
BF16 = jnp.bfloat16
F32 = jnp.float32
LANES = 128
SCALE = HEAD ** (-0.5)
VMEM_BYTES = 12 * 2**20
GRADS_VMEM_BYTES = 20 * 2**20


def turn(value, axis, steps):
    count = lax.axis_size(axis)
    return lax.ppermute(value, axis, [(i, (i + steps) % count) for i in range(count)])


def swap(value):
    return lax.ppermute(value, "section", [(0, 1), (1, 0)])


def contract(left, right, left_dim, right_dim):
    return lax.dot_general(
        left, right, (((left_dim,), (right_dim,)), ((), ())), preferred_element_type=F32
    )


def geometry(seq_lens, rows):
    count = lax.axis_size("tensor")
    place = (lax.axis_index("tensor") - jnp.arange(count, dtype=jnp.int32)) % count
    row_ids = (place[:, None] * rows + jnp.arange(rows, dtype=jnp.int32)[None, :]).reshape(-1)
    ends = jnp.cumsum(seq_lens)
    starts = ends - seq_lens
    member = jnp.sum((row_ids[:, None] >= ends[None, :]).astype(jnp.int32), axis=1)
    slots = jnp.arange(seq_lens.shape[0], dtype=jnp.int32)
    begins = jnp.sum(jnp.where(member[:, None] == slots[None, :], starts[None, :], 0), axis=1)
    position = row_ids - begins
    half_dim = HEAD // 2
    frequency = 10000.0 ** (-jnp.arange(half_dim, dtype=F32) / half_dim)
    angle = position.astype(F32)[:, None] * frequency[None, :]
    allowed = (member[:, None] == member[None, :]) & (row_ids[:, None] >= row_ids[None, :])
    cosine, sine_part = (jnp.cos(angle), jnp.sin(angle))
    cosine = jnp.concatenate([cosine] * (LANES // half_dim), axis=1)
    sine_part = jnp.concatenate([-sine_part, sine_part] * (LANES // HEAD), axis=1)
    turned = jnp.arange(LANES) < HEAD
    tables = jnp.stack(
        [cosine, sine_part, jnp.where(turned, cosine, 1.0), jnp.where(turned, sine_part, 0.0)]
    )
    return (tables, jnp.where(allowed, 0.0, MASK_FILL))


def barrier(*values):
    return lax.optimization_barrier(values)


class Job:
    def __init__(self, fn, *inputs, held=()):
        self.fn, self.inputs, self.held, self.results = (fn, inputs, held, None)

    def __getitem__(self, which):
        return self.results[which]


def step(value, job):
    if job is None:
        return turn(value, "tensor", 1)
    inputs = job.inputs() if callable(job.inputs) else job.inputs
    value, *inputs = barrier(value, *inputs)
    results = job.fn(*inputs)
    recv, *values = barrier(turn(value, "tensor", 1), *results, *job.held)
    job.results, job.held = (values[: len(results)], values[len(results) :])
    return recv


def spread(block, jobs=(), parts=1):
    pieces = list(jnp.split(block, parts))
    for k in range(lax.axis_size("tensor") - 1):
        for _ in range(parts):
            pieces.append(step(pieces[-parts], jobs[k] if k < len(jobs) else None))
    return jnp.concatenate(pieces, axis=0)


def collect(partial, jobs=()):
    count = lax.axis_size("tensor")
    rows = partial.shape[0] // count
    blocks = partial.reshape(count, rows, partial.shape[1])
    total = blocks[1 % count]
    for k in range(count - 1):
        recv = step(total.astype(BF16), jobs[k] if k < len(jobs) else None)
        total = recv.astype(F32) + blocks[(k + 2) % count].astype(F32)
    return total


class Ring:
    def __init__(self, first):
        self.count, self.taken, self.value = (lax.axis_size("tensor"), 0, first)

    def run(self, fn, *inputs):
        if self.taken == self.count - 1:
            return fn(*inputs)
        job = Job(fn, *inputs)
        self.accept(step(self.value, job))
        self.taken += 1
        return tuple(job.results)

    def finish(self):
        while self.taken < self.count - 1:
            self.run(lambda: ())
        return self.result()


class SpreadRing(Ring):
    def __init__(self, block):
        super().__init__(block)
        self.pieces = [block]

    def accept(self, recv):
        self.pieces.append(recv)
        self.value = recv

    def result(self):
        return jnp.concatenate(self.pieces, axis=0)


class CollectRing(Ring):
    def __init__(self, partial):
        count = lax.axis_size("tensor")
        self.blocks = partial.reshape(count, partial.shape[0] // count, partial.shape[1])
        self.total = self.blocks[1 % count].astype(F32)
        super().__init__(self.total.astype(BF16))

    def accept(self, recv):
        block = self.blocks[(self.taken + 2) % self.count]
        self.total = recv.astype(F32) + block.astype(F32)
        self.value = self.total.astype(BF16)

    def result(self):
        return self.total


def estimate(us):
    return pl.CostEstimate(flops=0, bytes_accessed=int(us * 3.3e6), transcendentals=0)


def normalizer(rows):
    return lax.rsqrt(jnp.mean(rows * rows, axis=1, keepdims=True) + EPSILON)


def half_swap(x):
    lane = lax.broadcasted_iota(jnp.int32, x.shape, 1)
    first = (lane % HEAD) < HEAD // 2
    return jnp.where(
        first, pltpu.roll(x, LANES - HEAD // 2, 1), pltpu.roll(x, HEAD // 2, 1)
    )


def heads_of(kv):
    low = lax.broadcasted_iota(jnp.int32, kv.shape, 1) < HEAD
    kv = kv.astype(F32)
    turned = pltpu.roll(kv, HEAD, 1)
    keys = (jnp.where(low, kv, 0.0).astype(BF16), jnp.where(low, 0.0, turned).astype(BF16))
    values = (jnp.where(low, turned, 0.0).astype(BF16), jnp.where(low, 0.0, kv).astype(BF16))
    return (keys, values)


def attend_kernel(qkv_ref, table_ref, bias_ref, rot_ref, mixed_ref, lse_ref):
    q_cols = mixed_ref.shape[1]
    cosine, sine_part = (table_ref[0], table_ref[1])
    kv = qkv_ref[:, q_cols:]
    kv = (kv * table_ref[2] + half_swap(kv) * table_ref[3]).astype(BF16)
    rot_ref[:, q_cols:] = kv
    keys, values = heads_of(kv)
    bias = bias_ref[...]
    head_ids = lax.broadcasted_iota(jnp.int32, lse_ref.shape, 1)

    def one_slab(slab, log_totals):
        cols = pl.ds(pl.multiple_of(slab * LANES, LANES), LANES)
        query = qkv_ref[:, cols]
        query = (query * cosine + half_swap(query) * sine_part).astype(BF16)
        rot_ref[:, cols] = query
        mixed = 0.0
        for odd in range(2):
            scores = contract(query, keys[odd], 1, 1) * SCALE + bias
            row_max = jnp.max(scores, axis=1, keepdims=True)
            exponent = jnp.exp(scores - row_max)
            totals = jnp.sum(exponent, axis=1, keepdims=True)
            log_total = row_max + jnp.log(totals)
            log_totals = jnp.where(head_ids == 2 * slab + odd, log_total, log_totals)
            mixed = mixed + contract((exponent / totals).astype(BF16), values[odd], 1, 0)
        mixed_ref[:, cols] = mixed.astype(BF16)
        return log_totals

    lse_ref[...] = lax.fori_loop(
        0, q_cols // LANES, one_slab, jnp.zeros(lse_ref.shape, F32)
    )


def attend(normed_one, geo, w_attn, q_cols, kv_cols):
    group = normed_one.shape[0]
    both = q_cols + 2 * kv_cols
    qkv = jnp.dot(normed_one, w_attn[:, :both], preferred_element_type=F32)
    rotated, mixed, log_total = pl.pallas_call(
        attend_kernel,
        out_shape=(
            jax.ShapeDtypeStruct((group, both), BF16),
            jax.ShapeDtypeStruct((group, q_cols), BF16),
            jax.ShapeDtypeStruct((group, q_cols // HEAD), F32),
        ),
        cost_estimate=estimate(3),
        compiler_params=pltpu.CompilerParams(vmem_limit_bytes=VMEM_BYTES),
    )(qkv, *geo)
    out_term = contract(mixed, w_attn[:, both : both + q_cols], 1, 1).astype(BF16)
    return (out_term, rotated, log_total, mixed)


def attend_back_kernel(d_mixed_ref, rot_ref, lse_ref, table_ref, bias_ref, out_ref):
    q_cols = d_mixed_ref.shape[1]
    cosine, sine_part = (table_ref[0], table_ref[1])
    keys, values = heads_of(rot_ref[:, q_cols:])
    bias = bias_ref[...]
    log_totals = lse_ref[...]
    head_ids = lax.broadcasted_iota(jnp.int32, log_totals.shape, 1)

    def one_slab(slab, sums):
        d_keys, d_values = (list(sums[:2]), list(sums[2:]))
        cols = pl.ds(pl.multiple_of(slab * LANES, LANES), LANES)
        query = rot_ref[:, cols]
        d_mixed = d_mixed_ref[:, cols]
        d_query = 0.0
        for odd in range(2):
            log_total = jnp.sum(
                jnp.where(head_ids == 2 * slab + odd, log_totals, 0.0), axis=1, keepdims=True
            )
            scores = contract(query, keys[odd], 1, 1) * SCALE + bias
            probs = jnp.exp(scores - log_total)
            d_probs = contract(d_mixed, values[odd], 1, 1)
            total = jnp.sum(d_probs * probs, axis=1, keepdims=True)
            d_scores = (probs * (d_probs - total)).astype(BF16)
            d_query = d_query + contract(d_scores, keys[odd], 1, 0)
            d_values[odd] = d_values[odd] + contract(probs.astype(BF16), d_mixed, 0, 0)
            d_keys[odd] = d_keys[odd] + contract(d_scores, query, 0, 0)
        d_query = d_query * SCALE
        out_ref[:, cols] = (d_query * cosine - half_swap(d_query) * sine_part).astype(BF16)
        return (*d_keys, *d_values)

    zeros = jnp.zeros((d_mixed_ref.shape[0], LANES), F32)
    sums = lax.fori_loop(0, q_cols // LANES, one_slab, (zeros,) * 4)
    d_keys, d_values = (sums[:2], sums[2:])
    low = lax.broadcasted_iota(jnp.int32, d_keys[0].shape, 1) < HEAD
    d_kv = jnp.where(
        low,
        (d_keys[0] + pltpu.roll(d_keys[1], HEAD, 1)) * SCALE,
        d_values[1] + pltpu.roll(d_values[0], HEAD, 1),
    )
    d_kv = d_kv * table_ref[2] - half_swap(d_kv) * table_ref[3]
    out_ref[:, q_cols:] = d_kv.astype(BF16)


def attend_back(grad_attn, geo, w_attn, at_first, rotated, log_total):
    other_attn = swap(core_half(grad_attn, at_first, False))
    both = rotated.shape[1]
    q_cols = log_total.shape[1] * HEAD
    w_out = w_attn[:, both : both + q_cols]
    d_mixed = jnp.dot(grad_attn, w_out, preferred_element_type=F32).astype(BF16)
    d_qkv = pl.pallas_call(
        attend_back_kernel,
        out_shape=jax.ShapeDtypeStruct(rotated.shape, BF16),
        cost_estimate=estimate(6),
        compiler_params=pltpu.CompilerParams(vmem_limit_bytes=VMEM_BYTES),
    )(d_mixed, rotated, log_total, *geo)
    d_norm_one = contract(d_qkv, w_attn[:, :both], 1, 1).astype(BF16)
    return (d_qkv, swap(d_qkv), other_attn, d_norm_one)


def feed(normed_two, w_ffn, units):
    gate_up = jnp.dot(normed_two, w_ffn[:, : 2 * units], preferred_element_type=F32)
    hidden = (jax.nn.silu(gate_up[:, :units]) * gate_up[:, units:]).astype(BF16)
    return (gate_up, hidden)


def feed_back(grad_feed, gate_up, w_ffn):
    units = gate_up.shape[1] // 2
    d_hidden = jnp.dot(grad_feed, w_ffn[:, 2 * units :], preferred_element_type=F32)
    gate, up = (gate_up[:, :units], gate_up[:, units:])
    sigmoid_gate = jax.nn.sigmoid(gate)
    d_up = (d_hidden * gate * sigmoid_gate).astype(BF16)
    d_gate = (d_hidden * up * sigmoid_gate * (1.0 + gate * (1.0 - sigmoid_gate))).astype(BF16)
    return (jnp.concatenate([d_gate, d_up], axis=1),)


def feed_back_rows(d_gate_up, w_ffn):
    return (contract(d_gate_up, w_ffn[:, : d_gate_up.shape[1]], 1, 1),)


def core_half(rows, at_first, own):
    width = rows.shape[1] // (2 * lax.axis_size("dp"))
    low, high = (
        jnp.concatenate(
            [rows[:, start : start + width] for start in range(first, rows.shape[1], 2 * width)],
            axis=1,
        )
        for first in (0, width)
    )
    return jnp.where(at_first, low, high) if own else jnp.where(at_first, high, low)


def exchange(at_first, rows, *whole):
    return tuple(swap(core_half(x, at_first, False)) for x in rows) + tuple(map(swap, whole))


def weight_grads_kernel(_, *refs):
    *pairs, out_ref = refs
    at = 0
    for k in range(0, len(pairs), 4):
        rows, other_rows, grads, other_grads = (ref[...] for ref in pairs[k : k + 4])
        total = contract(rows, grads, 0, 0) + contract(other_rows, other_grads, 0, 0)
        out_ref[:, at : at + total.shape[1]] = total.astype(BF16)
        at += total.shape[1]


def weight_grads(at_first, *pairs):
    group, half = pairs[0][1].shape
    n_dp = lax.axis_size("dp")
    tile = half // n_dp
    direct = tile % LANES == 0
    if not direct:
        pairs = [(core_half(rows, at_first, True), *rest) for rows, *rest in pairs]
        tile = min(256, half)
    specs = []
    for _, _, grads, _ in pairs:
        own_spec = pl.BlockSpec((group, tile), lambda i, core: (0, 2 * i + core[0]))
        half_spec = pl.BlockSpec((group, tile), lambda i, core: (0, i))
        grads_spec = pl.BlockSpec(
            (group, grads.shape[1]), lambda i, core: (0, 0), pipeline_mode=pl.Buffered(1)
        )
        specs += [own_spec if direct else half_spec, half_spec, grads_spec, grads_spec]
    total = sum(grads.shape[1] for _, _, grads, _ in pairs)
    return pl.pallas_call(
        weight_grads_kernel,
        grid_spec=pltpu.PrefetchScalarGridSpec(
            num_scalar_prefetch=1,
            grid=(half // tile,),
            in_specs=specs,
            out_specs=pl.BlockSpec((tile, total), lambda i, core: (i, 0)),
        ),
        out_shape=pltpu.HBM((half, total), BF16),
        cost_estimate=estimate(total / 330),
        compiler_params=pltpu.CompilerParams(vmem_limit_bytes=GRADS_VMEM_BYTES),
    )(
        jnp.where(at_first, 0, 1).astype(jnp.int32).reshape(1),
        *[x for pair in pairs for x in pair],
    )


def scatter(half):
    return lax.psum_scatter(half, "dp", scatter_dimension=0, tiled=True)


def norm_back(rows, inverse, gain, d_normed):
    unit = rows * inverse
    scaled = d_normed * gain
    return inverse * (scaled - unit * jnp.mean(scaled * unit, axis=1, keepdims=True))


def backward(
    kept, grad_all, grad, geo, weights, at_first, others, early, aside, down_job
):
    (layer_in, normed_one, rotated, log_total, mixed, middle, normed_two, gate_up, hidden) = kept
    norm_gain, ffn_gain, w_attn, w_ffn = weights
    last = down_job is None
    run = aside.run if aside else lambda fn, *inputs: fn(*inputs)
    (d_gate_up,) = run(feed_back, grad_all, gate_up, w_ffn)
    (d_norm_two_all,) = run(feed_back_rows, d_gate_up, w_ffn)
    if last:
        d_gate_up, grad_all = barrier(d_gate_up, grad_all)
        others["grad_all"] = exchange(at_first, (grad_all,))[0]

    def grads(*given):
        pairs = [given[k : k + 4] for k in range(0, len(given), 4)]
        return (weight_grads(at_first, *pairs),)

    if last:
        pairs = (
            *(normed_two, others["normed_two"], d_gate_up, swap(d_gate_up)),
            *(grad_all, others["grad_all"], hidden, others["hidden"]),
        )
        d_norm_two_all, *pairs = barrier(d_norm_two_all, *pairs)
        grads_jobs = (Job(grads, *pairs), Job(lambda: (), held=early))
        d_norm_two = collect(d_norm_two_all, grads_jobs)
        early = grads_jobs[1].held
    else:
        swap_job = Job(
            lambda d_gate_up, hidden, *rows: (
                swap(d_gate_up), swap(hidden), *exchange(at_first, rows)
            ),
            d_gate_up,
            hidden,
            normed_two,
            grad_all,
        )
        grads_jobs = (Job(grads),)
        grads_jobs[0].inputs = lambda: (normed_two, swap_job[2], d_gate_up, swap_job[0])
        d_norm_two = collect(d_norm_two_all, (swap_job, *grads_jobs))
    reduced = [scatter(job[0]) for job in grads_jobs if job.results]
    d_middle = grad.astype(F32) + norm_back(middle, normalizer(middle), ffn_gain, d_norm_two)
    ffn_gain_job = Job(
        lambda d_all, normed: (
            jnp.sum(d_all.astype(F32) * (normed.astype(F32) / ffn_gain), axis=0),
        ),
        d_norm_two_all,
        normed_two,
    )
    if last:
        aside_job = Job(lambda value: (turn(value, "tensor", 1),), aside.value)
        grad_attn = spread(d_middle.astype(BF16), (ffn_gain_job, aside_job))
        aside.accept(aside_job[0])
        aside.taken += 1
    else:
        down_grad = Job(grads, grad_all, swap_job[3], hidden, swap_job[1])
        grad_attn = spread(d_middle.astype(BF16), (down_grad, down_job, ffn_gain_job))
        reduced.append(scatter(down_grad[0]))
        aside = CollectRing(down_job[0])
    d_qkv, other_qkv, other_attn, d_norm_one_all = attend_back(
        grad_attn, geo, w_attn, at_first, rotated, log_total
    )
    other_one, other_mixed = others.get("attn") or exchange(at_first, (normed_one,), mixed)
    pairs = (
        *(normed_one, other_one, d_qkv, other_qkv),
        *(grad_attn, other_attn, mixed, other_mixed),
    )
    d_norm_one_all, *pairs = barrier(d_norm_one_all, *pairs)
    matrices = []

    def last_grads(*given):
        matrices.extend(grads(*given))
        return ()

    attn_job = Job(last_grads if last else grads, *pairs, held=reduced[:1] if last else ())
    attn_gain_job = Job(
        lambda d_all, normed: (
            jnp.sum(d_all.astype(F32) * (normed.astype(F32) / norm_gain), axis=0),
        ),
        d_norm_one_all,
        normed_one,
    )
    last_job = Job(lambda: (), held=() if last else reduced[:1])
    d_norm_one = collect(d_norm_one_all, (attn_job, attn_gain_job, last_job))
    reduced[:1] = attn_job.held or last_job.held
    r_attn = scatter(matrices[0] if last else attn_job[0])
    d_input = d_middle + norm_back(layer_in, normalizer(layer_in), norm_gain, d_norm_one)
    gain_grads = jnp.stack([attn_gain_job[0], ffn_gain_job[0]])
    return (d_input.astype(BF16), (r_attn, *reduced), gain_grads, early, aside)


def both_layers(own, at_first):
    rows = own.shape[0] // 2
    low, high = (own[:rows], own[rows:])
    mine = jnp.where(at_first, low, high)
    got = swap(jnp.where(at_first, high, low))
    return (jnp.where(at_first, mine, got), jnp.where(at_first, got, mine))


def own_layer(first, second, at_first):
    mine = jnp.where(at_first, first, second)
    got = swap(jnp.where(at_first, second, first))
    return jnp.concatenate([jnp.where(at_first, mine, got), jnp.where(at_first, got, mine)], axis=0)


def gather(shard):
    return lax.all_gather(shard, ("dp", "section"), axis=0, tiled=True)


def reduce_small(rows):
    for axis in ("tensor", "dp"):
        count = lax.axis_size(axis)
        if axis == "tensor":
            parts = rows.reshape(rows.shape[0], lax.axis_size("dp"), count, -1).transpose(2, 0, 1, 3)
        else:
            parts = rows.transpose(1, 0, 2)
        me = lax.axis_index(axis)
        rows = lax.dynamic_index_in_dim(parts, me, 0, keepdims=False)
        for k in range(1, count):
            part = lax.dynamic_index_in_dim(parts, (me + k) % count, 0, keepdims=False)
            rows = rows + turn(part, axis, k)
    return rows + swap(rows)


def local(
    tokens_in,
    cotangent,
    lengths,
    attn_gain,
    w_query,
    w_key,
    w_value,
    w_out,
    ffn_gain,
    w_gate,
    w_up,
    w_down,
):
    at_first = lax.axis_index("section") == 0
    rows = tokens_in.shape[1]
    q_cols, kv_cols, units = (w_query.shape[2], w_key.shape[2], w_gate.shape[2])
    tokens = jnp.where(at_first, tokens_in[0], tokens_in[1])
    upstream = jnp.where(at_first, cotangent[0], cotangent[1])
    gains_cols = jnp.pad(
        jnp.concatenate([attn_gain, ffn_gain], axis=0).T, ((0, 0), (0, LANES - 2))
    )
    attn_rows = jnp.concatenate(
        [w_query[0], w_key[0], w_value[0], w_out[0].T, gains_cols], axis=1
    )
    attn_rows, tokens = barrier(attn_rows, tokens)
    attn_parts = both_layers(attn_rows, at_first)
    prepare = Job(
        lambda gate, up, down: both_layers(
            jnp.concatenate([gate, up, down.T], axis=1), at_first
        ),
        w_gate[0],
        w_up[0],
        w_down[0],
    )
    tokens_all = spread(tokens, (None, prepare))
    tokens_all, upstream = barrier(tokens_all, upstream)
    upstream_ring = SpreadRing(upstream)
    first_attn = gather(attn_parts[0])
    first_ffn = gather(prepare[0])
    w_attns = [first_attn, gather(attn_parts[1])]
    w_ffns = [first_ffn]
    geo = geometry(jnp.where(at_first, lengths[0, 0], lengths[1, 0]), rows)
    tokens_all = tokens_all.astype(F32)
    layer_in = tokens.astype(F32)
    layers = []
    for layer in range(2):
        w_attn, w_ffn = (w_attns[layer], w_ffns[layer])
        norm_gain, ffn_gain = (
            w_attn[:, 2 * (q_cols + kv_cols) :][:, :2].T.astype(F32)
        )
        if layer:
            normed_one = spread(
                (layer_in * normalizer(layer_in) * norm_gain).astype(BF16), parts=2
            )
        else:
            normed_one = (tokens_all * normalizer(tokens_all) * norm_gain).astype(BF16)
        attention = (lambda normed, w: attend(normed, geo, w, q_cols, kv_cols), normed_one, w_attn)
        out_term, rotated, log_total, mixed = upstream_ring.run(*attention)
        others = {}
        attn_jobs = ()
        if layer == 0:
            ring_job = Job(lambda value: (turn(value, "tensor", 1),), upstream_ring.value)
            attn_jobs = (None, ring_job)
        middle = layer_in + collect(out_term, attn_jobs)
        normed_two = spread((middle * normalizer(middle) * ffn_gain).astype(BF16), parts=2)
        if layer == 0:
            upstream_ring.accept(ring_job[0])
            upstream_ring.taken += 1
            swapped = exchange(at_first, barrier(normed_one, normed_two)[:1], mixed)
            normed_two, *swapped = barrier(normed_two, *swapped)
            others.update(attn=tuple(swapped))
        gate_up, hidden = feed(normed_two, w_ffn, units)
        down_job = Job(
            lambda hidden, w: (contract(hidden, w[:, 2 * units :], 1, 1).astype(BF16),),
            hidden,
            w_ffn,
        )
        if layer == 0:
            (down_term,) = down_job.fn(*down_job.inputs)
            ffn_swap = Job(
                lambda two, units: exchange(at_first, (two,), units), normed_two, hidden
            )
            first_out = (middle + collect(down_term, (None, ffn_swap))).astype(BF16)
            others.update(normed_two=ffn_swap[0], hidden=ffn_swap[1])
            first_out, ffn_part = barrier(first_out, prepare[1])
            w_ffns.append(gather(ffn_part))
        kept = (
            layer_in, normed_one, rotated, log_total, mixed, middle, normed_two, gate_up, hidden
        )
        layers.append((kept, (norm_gain, ffn_gain, w_attn, w_ffn), others))
        layer_in = first_out.astype(F32)

    def back(layer, grad_all, grad, early, aside, down_job):
        kept, weights, others = layers[layer]
        return backward(
            kept,
            grad_all,
            grad,
            geo,
            weights,
            at_first,
            others,
            early,
            aside,
            down_job,
        )

    upstream_all = upstream_ring.finish()
    d_second, (second_attn, second_ffn, second_down), second_gains, _, out_ring = back(
        1, upstream_all, upstream, (), None, down_job
    )
    down_done = Job(lambda: (), held=(second_down,))
    d_second_all = spread(d_second, (None, down_done))
    d_first, (first_attn, first_ffn), first_gains, (second_attn,), _ = back(
        0, d_second_all, d_second, (second_attn,), out_ring, None
    )
    second_out = (middle + out_ring.finish()).astype(BF16)
    second_ffn = jnp.concatenate([second_ffn, *down_done.held], axis=1)
    g_gains = reduce_small(jnp.concatenate([first_gains, second_gains]))
    gain_own = jnp.where(at_first, g_gains[:2], g_gains[2:])

    def by_layer(first, second):
        mine = jnp.where(at_first, first, second)
        got = swap(jnp.where(at_first, second, first))
        return jnp.stack([jnp.where(at_first, mine, got), jnp.where(at_first, got, mine)])

    section_out = by_layer(first_out, second_out)
    input_grad = by_layer(d_first, d_second)
    g_ffn = own_layer(first_ffn, second_ffn, at_first).astype(F32)
    g_gate, g_up, g_down = (
        g_ffn[:, :units], g_ffn[:, units : 2 * units], g_ffn[:, 2 * units :].T
    )
    first_attn, gain_own, section_out, input_grad, g_gate, g_up, g_down = barrier(
        first_attn, gain_own, section_out, input_grad, g_gate, g_up, g_down
    )
    g_attn = own_layer(first_attn, second_attn, at_first).astype(F32)
    qkv = q_cols + 2 * kv_cols
    g_key_value = g_attn[:, q_cols:qkv].T
    return (
        section_out[None],
        input_grad[None],
        gain_own[0][None],
        g_attn[:, :q_cols][None],
        g_key_value[:kv_cols].T[None],
        g_key_value[kv_cols:].T[None],
        g_attn[:, qkv:].T[None],
        gain_own[1][None],
        g_gate[None],
        g_up[None],
        g_down[None],
    )


def solution(mesh):
    return jax.shard_map(
        local,
        mesh=mesh,
        in_specs=(
            P(None, ("dp", "tensor"), None),
            P(None, ("dp", "tensor"), None),
            P(None, "dp", None),
            P("section", "dp"),
            P("section", "dp", "tensor"),
            P("section", "dp", "tensor"),
            P("section", "dp", "tensor"),
            P("section", "tensor", "dp"),
            P("section", "dp"),
            P("section", "dp", "tensor"),
            P("section", "dp", "tensor"),
            P("section", "tensor", "dp"),
        ),
        out_specs=(
            P("section", None, ("dp", "tensor"), None),
            P("section", None, ("dp", "tensor"), None),
            P("section", ("dp", "tensor")),
            P("section", "dp", "tensor"),
            P("section", "dp", "tensor"),
            P("section", "dp", "tensor"),
            P("section", "tensor", "dp"),
            P("section", ("dp", "tensor")),
            P("section", "dp", "tensor"),
            P("section", "dp", "tensor"),
            P("section", "tensor", "dp"),
        ),
        check_vma=False,
    )
```
